256 devices in a mesh: layer: 2 (over x_lo), row: 4 (over x_hi, core), col: 32 (over y, z).
Axes of the slice: x: 4 (x_hi: 2, x_lo: 2; x = x_hi * 2 + x_lo), y: 4, z: 8, core: 2. Of those that a mesh axis runs over, the one named last changes fastest.
Arguments:
- ancestor: float32 [2, 8192, 8192], P('layer', 'row', 'col'), may hold values from -6 to 6
- lower_panels: float32 [2, 4, 512, 8192], P('layer', None, 'col', 'row'), may hold values from -6 to 6
- upper_panels: float32 [2, 4, 512, 8192], P('layer', None, 'row', 'col'), may hold values from -0.25 to 0.25
- lower_blocks: int32 [2, 4, 64], P('layer'), may hold values 0 or 1
- upper_blocks: int32 [2, 4, 64], P('layer'), may hold values 0 or 1
- final_lower: float32 [512, 8192], P(('layer', 'col'), 'row'), may hold values from -6 to 6
- final_upper: float32 [512, 8192], P(('layer', 'row'), 'col'), may hold values from -0.25 to 0.25
- final_lower_blocks: int32 [64], replicated, may hold values 0 or 1
- final_upper_blocks: int32 [64], replicated, may hold values 0 or 1
Outputs:
- summed: float32 [8192, 8192], P('row', 'col')
The draws below stay inside these ranges and needn't reach their ends.
All inputs are finite; a program needn't handle non-finite values. No bound on the sum of `lower_blocks` or of `upper_blocks` on one device may be relied on, other than what follows from the above.
Results may differ from the reference program's by a relative error of at most 0.0001.
Values sent between devices are 32-bit elements; how exact they have to be, the bound alone decides.
A program may use at most 128 MiB of HBM per device.

```python
import jax
import jax.numpy as jnp
from jax import lax

ORD = 8192
W = 512
BLK = 128
PANELS = 4
NB = 64
N_LAYER = 2


def place_ends(values, stream_key, smallest, high):
    longest = values.shape.index(max(values.shape))
    spots = []
    for shift in (0, 1):
        where = [jax.random.randint(jax.random.fold_in(stream_key, axis), (), 0, length) for axis, length in enumerate(values.shape)]
        where[longest] = (where[longest] + shift) % values.shape[longest]
        spots.append(tuple(where))
    return values.at[spots[0]].set(smallest).at[spots[1]].set(high)


def steps_of(key, extent, split, low, largest):
    def one(position, parts):
        steps = jax.random.uniform(jax.random.fold_in(jax.random.fold_in(key, 6), position), (parts,), jnp.float32, low / len(split), largest / len(split))
        return jnp.repeat(jnp.exp(steps), extent[position] // parts).reshape((-1,) + (1,) * (len(extent) - position - 1))

    factor_of = one(*split[0])
    for cut in split[1:]:
        factor_of = factor_of * one(*cut)
    return factor_of


def bell_draw(stream_key, extent, width, most, pieces=(), held_as=jnp.bfloat16):
    entries = jax.random.normal(stream_key, extent, jnp.float32) * width
    if len(pieces) > 0:
        entries = steps_of(stream_key, extent, pieces, -0.22, 0.18) * entries
    return jnp.clip(entries, min=-most, max=most).astype(held_as)


def setup_inputs(seed: int = 0) -> dict:
    arg_keys = jax.random.split(jax.random.key(seed), 10)
    return {
        "ancestor": bell_draw(arg_keys[0], (N_LAYER, ORD, ORD), 1.0, 6.0, ((0, 2), (1, 4), (2, 32)), jnp.float32),
        "lower_panels": bell_draw(arg_keys[1], (N_LAYER, PANELS, W, ORD), 1.0, 6.0, ((0, 2), (2, 32), (3, 4)), jnp.float32),
        "upper_panels": bell_draw(arg_keys[2], (N_LAYER, PANELS, W, ORD), W ** -0.5, 0.25, ((0, 2), (2, 4), (3, 32)), jnp.float32),
        "lower_blocks": place_ends((jax.random.randint(arg_keys[3], (N_LAYER, PANELS, NB), 0, 2) < 1).astype(jnp.int32), jax.random.fold_in(arg_keys[3], 1), 0, 1),
        "upper_blocks": place_ends((jax.random.randint(arg_keys[4], (N_LAYER, PANELS, NB), 0, 2) < 1).astype(jnp.int32), jax.random.fold_in(arg_keys[4], 1), 0, 1),
        "final_lower": bell_draw(arg_keys[5], (W, ORD), 1.0, 6.0, ((0, 64), (1, 4)), jnp.float32),
        "final_upper": bell_draw(arg_keys[6], (W, ORD), W ** -0.5, 0.25, ((0, 8), (1, 32)), jnp.float32),
        "final_lower_blocks": place_ends((jax.random.randint(arg_keys[7], (NB,), 0, 2) < 1).astype(jnp.int32), jax.random.fold_in(arg_keys[7], 1), 0, 1),
        "final_upper_blocks": place_ends((jax.random.randint(arg_keys[8], (NB,), 0, 2) < 1).astype(jnp.int32), jax.random.fold_in(arg_keys[8], 1), 0, 1),
    }


def expand(blocks):
    return jnp.repeat(blocks.astype(jnp.float32), BLK, axis=-1)


def contract(lower_masked, upper_masked):
    return lax.dot_general(lower_masked, upper_masked, (((0,), (0,)), ((), ())), precision=lax.Precision.HIGHEST, preferred_element_type=jnp.float32)


def reference(ancestor, lower_panels, upper_panels, lower_blocks, upper_blocks, final_lower, final_upper, final_lower_blocks, final_upper_blocks):
    summed = jnp.zeros((ORD, ORD), jnp.float32)
    for layer_index in range(N_LAYER):
        layer_part = ancestor[layer_index]
        for panel in range(PANELS):
            lower_masked = lower_panels[layer_index, panel] * expand(lower_blocks[layer_index, panel])[None, :]
            upper_masked = upper_panels[layer_index, panel] * expand(upper_blocks[layer_index, panel])[None, :]
            layer_part = layer_part - contract(lower_masked, upper_masked)
        summed = summed + layer_part
    lower_masked = final_lower * expand(final_lower_blocks)[None, :]
    upper_masked = final_upper * expand(final_upper_blocks)[None, :]
    return summed - contract(lower_masked, upper_masked)
```

```python
import jax
import jax.numpy as jnp
from jax import lax
from jax.experimental import pallas as pl
from jax.experimental.pallas import tpu as pltpu
from jax.sharding import PartitionSpec as P

BLK = 128
PANELS = 4
NY, NZ = 4, 8
ROWS = 4
R = 2
MESH = pl.DeviceIdType.MESH
F32, BF16 = jnp.float32, jnp.bfloat16


def split(value):
    high = value.astype(BF16)
    return high, (value - high.astype(F32)).astype(BF16)


def contract(lower, upper_high, upper_low):
    high, low = split(lower)

    def dot(a, b):
        return lax.dot_general(a, b, (((0,), (0,)), ((), ())), preferred_element_type=F32)

    return dot(high, upper_high) + dot(high, upper_low) + dot(low, upper_high)


def kernel(
    anc_ref, low_ref, up_ref, lb_ref, ub_ref, fl_ref, fu_ref, flb_ref, fub_ref,
    out_ref,
    ga, gb, ug, uh, ul, fh, flo, anc, mine, rx,
    s_a1, r_a1, s_a2, r_a2, s_b1, r_b1, s_b2, r_b2, s_u, r_u, s_x, r_x, l_anc, l_out,
):
    chunks = ga.shape[0]
    layer = lax.axis_index("layer")
    row = lax.axis_index("row")
    col = lax.axis_index("col")
    y, z = col // NZ, lax.rem(col, NZ)
    sib = row + 1 - 2 * lax.rem(row, 2)
    far = lax.rem(row + 2, ROWS)

    def at_y(d):
        return lax.rem(y + d + NY, NY)

    def at_z(d):
        return lax.rem(z + d + NZ, NZ)

    def col_of(yy, zz):
        return {"col": yy * NZ + zz}

    def remote(ref, ssem, rsem, target):
        return pltpu.make_async_remote_copy(
            src_ref=ref, dst_ref=ref, send_sem=ssem, recv_sem=rsem,
            device_id=target, device_id_type=MESH,
        )

    half_a = {1: (0, 40), -1: (40, 40)}
    half_b = {1: (0, 32), -1: (32, 32)}

    def a1(c, d, h, arriving):
        zz = at_z(-d * (h if arriving else h - 1))
        ref = ga.at[c, y, zz]
        if h == 4:
            ref = ga.at[c, y, zz, pl.ds(*half_a[d]), :]
        k = (0 if d == 1 else 4) + h - 1
        return remote(ref, s_a1.at[c, k], r_a1.at[c, k], col_of(y, at_z(d)))

    def a2(c, d, h, arriving):
        yy = at_y(-d * (h if arriving else h - 1))
        ref = ga.at[c, yy]
        if h == 2:
            ref = ga.at[c, yy, pl.ds(0 if d == 1 else NZ // 2, NZ // 2)]
        k = (0 if d == 1 else 2) + h - 1
        return remote(ref, s_a2.at[c, k], r_a2.at[c, k], col_of(at_y(d), z))

    def b1(c, d, h, arriving):
        yy = at_y(-d * (h if arriving else h - 1))
        ref = gb.at[c, z, yy]
        if h == 2:
            ref = gb.at[c, z, yy, pl.ds(*half_b[d]), :]
        k = (0 if d == 1 else 2) + h - 1
        return remote(ref, s_b1.at[c, k], r_b1.at[c, k], col_of(at_y(d), z))

    def b2(c, d, h, arriving):
        zz = at_z(-d * (h if arriving else h - 1))
        ref = gb.at[c, zz]
        if h == 4:
            ref = gb.at[c, zz, pl.ds(0 if d == 1 else NY // 2, NY // 2)]
        k = (0 if d == 1 else 4) + h - 1
        return remote(ref, s_b2.at[c, k], r_b2.at[c, k], col_of(y, at_z(d)))

    def begin(what, c):
        for d in (1, -1):
            what(c, d, 1, False).start()

    def forward(what, c, h):
        for d in (1, -1):
            what(c, d, h, True).wait_recv()
            what(c, d, h + 1, False).start()

    def arrive(what, c, h):
        for d in (1, -1):
            what(c, d, h, True).wait_recv()

    def sent(what, c, hops):
        for d in (1, -1):
            for h in range(1, hops + 1):
                what(c, d, h, False).wait_send()

    u_own_sib = remote(ug.at[row], s_u.at[0], r_u.at[0], {"row": sib})
    u_own_far = remote(ug.at[row], s_u.at[1], r_u.at[1], {"row": far})
    u_fwd = remote(ug.at[far], s_u.at[2], r_u.at[2], {"row": sib})
    far_sib = lax.rem(sib + 2, ROWS)

    def u_arrive(k, which):
        remote(ug.at[which], s_u.at[k], r_u.at[k], {"row": sib}).wait_recv()

    def exchange(c):
        return pltpu.make_async_remote_copy(
            src_ref=mine.at[c], dst_ref=rx.at[c], send_sem=s_x.at[c], recv_sem=r_x.at[c],
            device_id={"layer": 1 - layer}, device_id_type=MESH,
        )

    def store_out(c):
        return pltpu.make_async_copy(rx.at[c], out_ref.at[c], l_out.at[c])

    load_anc = pltpu.make_async_copy(anc_ref.at[0], anc, l_anc)
    load_anc.start()

    barrier = pltpu.get_barrier_semaphore()
    greeted = [
        {"row": sib}, {"row": far}, {"layer": 1 - layer},
        col_of(at_y(1), z), col_of(at_y(-1), z), col_of(y, at_z(1)), col_of(y, at_z(-1)),
    ]
    for other in greeted:
        pl.semaphore_signal(barrier, inc=1, device_id=other, device_id_type=MESH)

    for panel in range(PANELS):
        ug[row, panel * 128 : panel * 128 + 128, :] = up_ref[0, panel]
    ug[row, PANELS * 128 :, :] = fu_ref[...]

    def place(c, _):
        for r in range(R):
            lanes = pl.ds(pl.multiple_of((c * R + r) * BLK, BLK), BLK)
            for panel in range(PANELS):
                piece = low_ref[0, panel, :, lanes]
                where = pl.ds((panel % 2) * 16 * R + r * 16, 16)
                if panel < 2:
                    ga[c, y, z, where, :] = piece
                else:
                    gb[c, z, y, where, :] = piece
            ga[c, y, z, pl.ds(32 * R + r * 8, 8), :] = fl_ref[:, lanes]
        return 0

    lax.fori_loop(0, chunks, place, 0)
    pl.semaphore_wait(barrier, len(greeted))

    u_own_far.start()
    u_own_sib.start()

    def scale(mask_ref, *index):
        return mask_ref[index].astype(F32)

    def prepare_upper():
        u_arrive(0, sib)
        u_arrive(1, far)
        u_fwd.start()
        u_arrive(2, far_sib)
        for half in range(2):
            cols = slice(half * BLK, half * BLK + BLK)
            for panel in range(PANELS):
                keep = scale(ub_ref, 0, panel, col * 2 + half)
                if panel < 2:
                    for r in range(ROWS):
                        high, low = split(ug[r, panel * 128 : panel * 128 + 128, cols] * keep)
                        uh[panel, r * 128 : r * 128 + 128, cols] = high
                        ul[panel, r * 128 : r * 128 + 128, cols] = low
                else:
                    for source in range(NY * NZ):
                        sy, sz = source // NZ, source % NZ
                        r, at = source // 8, source % 8 * 16
                        to = (sz * NY + sy) * 16
                        high, low = split(
                            ug[r, panel * 128 + at : panel * 128 + at + 16, cols] * keep
                        )
                        uh[panel, to : to + 16, cols] = high
                        ul[panel, to : to + 16, cols] = low
            keep = scale(fub_ref, col * 2 + half)
            for r in range(ROWS):
                high, low = split(ug[r, PANELS * 128 :, cols] * keep)
                fh[r * 64 : r * 64 + 64, cols] = high
                flo[r * 64 : r * 64 + 64, cols] = low

    def compute(c, r):
        block = c * R + r
        rows = pl.ds(pl.multiple_of(block * BLK, BLK), BLK)
        total = anc[rows, :]
        for panel in range(PANELS):
            where = pl.ds((panel % 2) * 16 * R + r * 16, 16)
            held = ga if panel < 2 else gb
            piece = held[c, :, :, where, :].reshape(512, BLK)
            piece = piece * scale(lb_ref, 0, panel, row * 16 + block)
            total = total - contract(piece, uh[panel], ul[panel])
        piece = ga[c, :, :, pl.ds(32 * R + r * 8, 8), :].reshape(256, BLK)
        piece = piece * scale(flb_ref, row * 16 + block)
        total = total - contract(piece, fh[...], flo[...])
        mine[c, r * BLK : r * BLK + BLK, :] = total

    def finish(c):
        exchange(c).wait_recv()
        rx[c] = rx[c] + mine[c]
        store_out(c).start()

    def step(i, _):
        first = i < chunks
        second = (i >= 1) & (i <= chunks)
        third = i >= 2
        j = i - 1
        k = i - 2

        @pl.when(first)
        def _():
            begin(a1, i)
            begin(b1, i)

        @pl.when(second)
        def _():
            begin(a2, j)
            begin(b2, j)

        @pl.when(first)
        def _():
            forward(a1, i, 1)
            forward(b1, i, 1)
            forward(a1, i, 2)
            forward(a1, i, 3)

        @pl.when(i == 0)
        def _():
            load_anc.wait()

        @pl.when(i == 2)
        def _():
            prepare_upper()

        @pl.when(second)
        def _():
            forward(b2, j, 1)

        @pl.when(third)
        def _():
            arrive(a2, k, 2)
            arrive(b2, k, 4)
            compute(k, 0)

        @pl.when(second)
        def _():
            forward(a2, j, 1)
            forward(b2, j, 2)

        @pl.when(third)
        def _():
            compute(k, 1)
            exchange(k).start()
            sent(a1, k, 4)
            sent(b1, k, 2)
            sent(a2, k, 2)
            sent(b2, k, 4)

        @pl.when(second)
        def _():
            forward(b2, j, 3)

        @pl.when(i >= 3)
        def _():
            finish(i - 3)

        @pl.when(first)
        def _():
            arrive(a1, i, 4)
            arrive(b1, i, 2)

        return 0

    lax.fori_loop(0, chunks + 2, step, 0)
    finish(chunks - 1)
    u_own_sib.wait_send()
    u_own_far.wait_send()
    u_fwd.wait_send()

    def drain(c, _):
        exchange(c).wait_send()
        store_out(c).wait()
        return 0

    lax.fori_loop(0, chunks, drain, 0)


def body(anc, low, up, lb, ub, fl, fu, flb, fub):
    rows, cols = anc.shape[1:]
    chunks = rows // BLK // R
    vmem = pl.BlockSpec(memory_space=pltpu.VMEM)
    smem = pl.BlockSpec(memory_space=pltpu.SMEM)
    hbm = pl.BlockSpec(memory_space=pl.ANY)
    dma = pltpu.SemaphoreType.DMA
    out = pl.pallas_call(
        kernel,
        out_shape=jax.ShapeDtypeStruct((chunks, R * BLK, cols), F32),
        in_specs=[hbm, vmem, vmem, smem, smem, vmem, vmem, smem, smem],
        out_specs=hbm,
        scratch_shapes=[
            pltpu.VMEM((chunks, NY, NZ, 40 * R, BLK), F32),
            pltpu.VMEM((chunks, NZ, NY, 32 * R, BLK), F32),
            pltpu.VMEM((ROWS, PANELS * 128 + 64, cols), F32),
            pltpu.VMEM((PANELS, 512, cols), BF16),
            pltpu.VMEM((PANELS, 512, cols), BF16),
            pltpu.VMEM((256, cols), BF16),
            pltpu.VMEM((256, cols), BF16),
            pltpu.VMEM((rows, cols), F32),
            pltpu.VMEM((chunks, R * BLK, cols), F32),
            pltpu.VMEM((chunks, R * BLK, cols), F32),
            dma((chunks, 8)), dma((chunks, 8)),
            dma((chunks, 4)), dma((chunks, 4)),
            dma((chunks, 4)), dma((chunks, 4)),
            dma((chunks, 8)), dma((chunks, 8)),
            dma((3,)), dma((3,)),
            dma((chunks,)), dma((chunks,)),
            dma, dma((chunks,)),
        ],
        compiler_params=pltpu.CompilerParams(
            collective_id=0, has_side_effects=True, vmem_limit_bytes=56 << 20
        ),
        name="gather_update_exchange",
    )(anc, low, up, lb, ub, fl, fu, flb, fub)
    return out.reshape(rows, cols)


def solution(mesh):
    return jax.shard_map(
        body,
        mesh=mesh,
        in_specs=(
            P("layer", "row", "col"),
            P("layer", None, "col", "row"),
            P("layer", None, "row", "col"),
            P("layer", None, None),
            P("layer", None, None),
            P(("layer", "col"), "row"),
            P(("layer", "row"), "col"),
            P(),
            P(),
        ),
        out_specs=P("row", "col"),
        check_vma=False,
    )
```

```python
import jax
import jax.numpy as jnp
from jax import lax
from jax.experimental import pallas as pl
from jax.experimental.pallas import tpu as pltpu
from jax.sharding import PartitionSpec as P

BLK = 128
PANELS = 4
NY, NZ = 4, 8
ROWS = 4
R = 2
MESH = pl.DeviceIdType.MESH
F32, BF16 = jnp.float32, jnp.bfloat16


def split(value):
    high = value.astype(BF16)
    return high, (value - high.astype(F32)).astype(BF16)


def contract(lower, upper_high, upper_low):
    high, low = split(lower)

    def dot(a, b):
        return lax.dot_general(a, b, (((0,), (0,)), ((), ())), preferred_element_type=F32)

    return dot(high, upper_high) + dot(high, upper_low) + dot(low, upper_high)


def kernel(
    anc_ref, low_ref, up_ref, lb_ref, ub_ref, fl_ref, fu_ref, flb_ref, fub_ref,
    out_ref,
    ga, gb, ug, uh, ul, fh, flo, anc, mine, rx,
    s_a1, r_a1, s_a2, r_a2, s_b1, r_b1, s_b2, r_b2, s_u, r_u, s_x, r_x, l_anc, l_out,
):
    chunks = ga.shape[0]
    layer = lax.axis_index("layer")
    row = lax.axis_index("row")
    col = lax.axis_index("col")
    y, z = col // NZ, lax.rem(col, NZ)
    sib = row + 1 - 2 * lax.rem(row, 2)
    far = lax.rem(row + 2, ROWS)

    def at_y(d):
        return lax.rem(y + d + NY, NY)

    def at_z(d):
        return lax.rem(z + d + NZ, NZ)

    def col_of(yy, zz):
        return {"col": yy * NZ + zz}

    def remote(ref, ssem, rsem, target):
        return pltpu.make_async_remote_copy(
            src_ref=ref, dst_ref=ref, send_sem=ssem, recv_sem=rsem,
            device_id=target, device_id_type=MESH,
        )

    half_a = {1: (0, 40 * R // 16 * 8), -1: (40 * R // 16 * 8, 40 * R - 40 * R // 16 * 8)}
    half_b = {1: (0, 16 * R), -1: (16 * R, 16 * R)}

    def a1(c, d, h, arriving):
        zz = at_z(-d * (h if arriving else h - 1))
        ref = ga.at[c, y, zz]
        if h == 4:
            ref = ga.at[c, y, zz, pl.ds(*half_a[d]), :]
        k = (0 if d == 1 else 4) + h - 1
        return remote(ref, s_a1.at[c, k], r_a1.at[c, k], col_of(y, at_z(d)))

    def a2(c, d, h, arriving):
        yy = at_y(-d * (h if arriving else h - 1))
        ref = ga.at[c, yy]
        if h == 2:
            ref = ga.at[c, yy, pl.ds(0 if d == 1 else NZ // 2, NZ // 2)]
        k = (0 if d == 1 else 2) + h - 1
        return remote(ref, s_a2.at[c, k], r_a2.at[c, k], col_of(at_y(d), z))

    def b1(c, d, h, arriving):
        yy = at_y(-d * (h if arriving else h - 1))
        ref = gb.at[c, z, yy]
        if h == 2:
            ref = gb.at[c, z, yy, pl.ds(*half_b[d]), :]
        k = (0 if d == 1 else 2) + h - 1
        return remote(ref, s_b1.at[c, k], r_b1.at[c, k], col_of(at_y(d), z))

    def b2(c, d, h, arriving):
        zz = at_z(-d * (h if arriving else h - 1))
        ref = gb.at[c, zz]
        if h == 4:
            ref = gb.at[c, zz, pl.ds(0 if d == 1 else NY // 2, NY // 2)]
        k = (0 if d == 1 else 4) + h - 1
        return remote(ref, s_b2.at[c, k], r_b2.at[c, k], col_of(y, at_z(d)))

    def begin(what, c):
        for d in (1, -1):
            what(c, d, 1, False).start()

    def forward(what, c, h):
        for d in (1, -1):
            what(c, d, h, True).wait_recv()
            what(c, d, h + 1, False).start()

    def arrive(what, c, h):
        for d in (1, -1):
            what(c, d, h, True).wait_recv()

    def sent(what, c, hops):
        for d in (1, -1):
            for h in range(1, hops + 1):
                what(c, d, h, False).wait_send()

    u_own_sib = remote(ug.at[row], s_u.at[0], r_u.at[0], {"row": sib})
    u_own_far = remote(ug.at[row], s_u.at[1], r_u.at[1], {"row": far})
    u_fwd = remote(ug.at[far], s_u.at[2], r_u.at[2], {"row": sib})
    far_sib = lax.rem(sib + 2, ROWS)

    def u_arrive(k, which):
        remote(ug.at[which], s_u.at[k], r_u.at[k], {"row": sib}).wait_recv()

    def exchange(c):
        return pltpu.make_async_remote_copy(
            src_ref=mine.at[c], dst_ref=rx.at[c], send_sem=s_x.at[c], recv_sem=r_x.at[c],
            device_id={"layer": 1 - layer}, device_id_type=MESH,
        )

    def store_out(c):
        return pltpu.make_async_copy(rx.at[c], out_ref.at[c], l_out.at[c])

    load_anc = pltpu.make_async_copy(anc_ref.at[0], anc, l_anc)
    load_anc.start()

    barrier = pltpu.get_barrier_semaphore()
    greeted = [
        {"row": sib}, {"row": far}, {"layer": 1 - layer},
        col_of(at_y(1), z), col_of(at_y(-1), z), col_of(y, at_z(1)), col_of(y, at_z(-1)),
    ]
    for other in greeted:
        pl.semaphore_signal(barrier, inc=1, device_id=other, device_id_type=MESH)

    for panel in range(PANELS):
        ug[row, panel * 128 : panel * 128 + 128, :] = up_ref[0, panel]
    ug[row, PANELS * 128 :, :] = fu_ref[...]

    def place(c, _):
        for r in range(R):
            lanes = pl.ds(pl.multiple_of((c * R + r) * BLK, BLK), BLK)
            for panel in range(PANELS):
                piece = low_ref[0, panel, :, lanes]
                where = pl.ds((panel % 2) * 16 * R + r * 16, 16)
                if panel < 2:
                    ga[c, y, z, where, :] = piece
                else:
                    gb[c, z, y, where, :] = piece
            ga[c, y, z, pl.ds(32 * R + r * 8, 8), :] = fl_ref[:, lanes]
        return 0

    lax.fori_loop(0, chunks, place, 0)
    pl.semaphore_wait(barrier, len(greeted))

    u_own_far.start()
    u_own_sib.start()

    def scale(mask_ref, *index):
        return mask_ref[index].astype(F32)

    def prepare_upper():
        u_arrive(0, sib)
        u_arrive(1, far)
        u_fwd.start()
        u_arrive(2, far_sib)
        for half in range(2):
            cols = slice(half * BLK, half * BLK + BLK)
            for panel in range(PANELS):
                keep = scale(ub_ref, 0, panel, col * 2 + half)
                if panel < 2:
                    for r in range(ROWS):
                        high, low = split(ug[r, panel * 128 : panel * 128 + 128, cols] * keep)
                        uh[panel, r * 128 : r * 128 + 128, cols] = high
                        ul[panel, r * 128 : r * 128 + 128, cols] = low
                else:
                    for source in range(NY * NZ):
                        sy, sz = source // NZ, source % NZ
                        r, at = source // 8, source % 8 * 16
                        to = (sz * NY + sy) * 16
                        high, low = split(
                            ug[r, panel * 128 + at : panel * 128 + at + 16, cols] * keep
                        )
                        uh[panel, to : to + 16, cols] = high
                        ul[panel, to : to + 16, cols] = low
            keep = scale(fub_ref, col * 2 + half)
            for r in range(ROWS):
                high, low = split(ug[r, PANELS * 128 :, cols] * keep)
                fh[r * 64 : r * 64 + 64, cols] = high
                flo[r * 64 : r * 64 + 64, cols] = low

    def compute(c, r):
        block = c * R + r
        rows = pl.ds(pl.multiple_of(block * BLK, BLK), BLK)
        total = anc[rows, :]
        for panel in range(PANELS):
            where = pl.ds((panel % 2) * 16 * R + r * 16, 16)
            held = ga if panel < 2 else gb
            piece = held[c, :, :, where, :].reshape(512, BLK)
            piece = piece * scale(lb_ref, 0, panel, row * 16 + block)
            total = total - contract(piece, uh[panel], ul[panel])
        piece = ga[c, :, :, pl.ds(32 * R + r * 8, 8), :].reshape(256, BLK)
        piece = piece * scale(flb_ref, row * 16 + block)
        total = total - contract(piece, fh[...], flo[...])
        mine[c, r * BLK : r * BLK + BLK, :] = total

    def finish(c):
        exchange(c).wait_recv()
        rx[c] = rx[c] + mine[c]
        store_out(c).start()

    def upper(c):
        @pl.when(c == 0)
        def _():
            load_anc.wait()
            prepare_upper()

    def work(c):
        for r in range(R):
            compute(c, r)
        exchange(c).start()

    def clear(c):
        sent(a1, c, 4)
        sent(b1, c, 2)
        sent(a2, c, 2)
        sent(b2, c, 4)

    def starts(what):
        return lambda c: begin(what, c)

    def moves(what, hop):
        return lambda c: forward(what, c, hop)

    def ends(what, hop):
        return lambda c: arrive(what, c, hop)

    def step(i, _):
        def run(offset, *actions):
            @pl.when((i >= offset) & (i < chunks + offset))
            def _():
                for action in actions:
                    action(i - offset)

        run(0, starts(a1), starts(b1))
        run(1, moves(a1, 1), moves(b1, 1))
        run(2, moves(a1, 2), ends(b1, 2), starts(b2))
        run(3, moves(a1, 3), moves(b2, 1))
        run(4, ends(a1, 4), starts(a2), moves(b2, 2))
        run(5, moves(a2, 1), moves(b2, 3))
        run(6, upper, ends(a2, 2), ends(b2, 4), work)
        run(7, clear, finish)
        return 0

    lax.fori_loop(0, chunks + 8, step, 0)
    u_own_sib.wait_send()
    u_own_far.wait_send()
    u_fwd.wait_send()

    def drain(c, _):
        exchange(c).wait_send()
        store_out(c).wait()
        return 0

    lax.fori_loop(0, chunks, drain, 0)


def body(anc, low, up, lb, ub, fl, fu, flb, fub):
    rows, cols = anc.shape[1:]
    chunks = rows // BLK // R
    vmem = pl.BlockSpec(memory_space=pltpu.VMEM)
    smem = pl.BlockSpec(memory_space=pltpu.SMEM)
    hbm = pl.BlockSpec(memory_space=pl.ANY)
    dma = pltpu.SemaphoreType.DMA
    out = pl.pallas_call(
        kernel,
        out_shape=jax.ShapeDtypeStruct((chunks, R * BLK, cols), F32),
        in_specs=[hbm, vmem, vmem, smem, smem, vmem, vmem, smem, smem],
        out_specs=hbm,
        scratch_shapes=[
            pltpu.VMEM((chunks, NY, NZ, 40 * R, BLK), F32),
            pltpu.VMEM((chunks, NZ, NY, 32 * R, BLK), F32),
            pltpu.VMEM((ROWS, PANELS * 128 + 64, cols), F32),
            pltpu.VMEM((PANELS, 512, cols), BF16),
            pltpu.VMEM((PANELS, 512, cols), BF16),
            pltpu.VMEM((256, cols), BF16),
            pltpu.VMEM((256, cols), BF16),
            pltpu.VMEM((rows, cols), F32),
            pltpu.VMEM((chunks, R * BLK, cols), F32),
            pltpu.VMEM((chunks, R * BLK, cols), F32),
            dma((chunks, 8)), dma((chunks, 8)),
            dma((chunks, 4)), dma((chunks, 4)),
            dma((chunks, 4)), dma((chunks, 4)),
            dma((chunks, 8)), dma((chunks, 8)),
            dma((3,)), dma((3,)),
            dma((chunks,)), dma((chunks,)),
            dma, dma((chunks,)),
        ],
        compiler_params=pltpu.CompilerParams(
            collective_id=0, has_side_effects=True, vmem_limit_bytes=56 << 20
        ),
        name="gather_update_exchange",
    )(anc, low, up, lb, ub, fl, fu, flb, fub)
    return out.reshape(rows, cols)


def solution(mesh):
    return jax.shard_map(
        body,
        mesh=mesh,
        in_specs=(
            P("layer", "row", "col"),
            P("layer", None, "col", "row"),
            P("layer", None, "row", "col"),
            P("layer", None, None),
            P("layer", None, None),
            P(("layer", "col"), "row"),
            P(("layer", "row"), "col"),
            P(),
            P(),
        ),
        out_specs=P("row", "col"),
        check_vma=False,
    )
```

```python
import functools

import jax
import jax.numpy as jnp
from jax import lax
from jax.experimental import pallas as pl
from jax.experimental.pallas import tpu as pltpu
from jax.sharding import PartitionSpec as P

BLK = 128
PANELS = 4
NY, NZ = 4, 8
ROWS = 4
R = 2
CHUNKS = 8
TILES = 9
BLOCKS = 16
SIZES = ((11, 7), (12, 7), (18, 11))
T_OF, ORDER, SOURCE, POS, POS_OTHER, MOST = 0, 9, 10, 12, 13, 14
MESH = pl.DeviceIdType.MESH
F32, BF16 = jnp.float32, jnp.bfloat16


def split(value):
    high = value.astype(BF16)
    return high, (value - high.astype(F32)).astype(BF16)


def contract(high, low, upper_high, upper_low):

    def dot(a, b):
        return lax.dot_general(a, b, (((0,), (0,)), ((), ())), preferred_element_type=F32)

    return dot(high, upper_high) + dot(high, upper_low) + dot(low, upper_high)


def kernel(
    tiles, tiles_a, tab_ref, anc_ref, low_ref, up_ref, ub_ref, fl_ref, fu_ref, fub_ref,
    mine_ref, rx_ref,
    gathered, own, high, low, ug, uh, ul, anc, mine,
    s_a1, r_a1, s_a2, r_a2, s_b1, r_b1, s_b2, r_b2, s_u, r_u, s_x, r_x, l_anc, l_out,
):
    chunks = CHUNKS
    tiles_b = tiles - tiles_a
    layer = lax.axis_index("layer")
    row = lax.axis_index("row")
    col = lax.axis_index("col")
    y, z = col // NZ, lax.rem(col, NZ)
    sib = row + 1 - 2 * lax.rem(row, 2)
    far = lax.rem(row + 2, ROWS)

    def at_y(d):
        return lax.rem(y + d + NY, NY)

    def at_z(d):
        return lax.rem(z + d + NZ, NZ)

    def col_of(yy, zz):
        return {"col": yy * NZ + zz}

    def remote(ref, ssem, rsem, target):
        return pltpu.make_async_remote_copy(
            src_ref=ref, dst_ref=ref, send_sem=ssem, recv_sem=rsem,
            device_id=target, device_id_type=MESH,
        )

    def halved(d, first, count):
        cut = count // 2
        return (first, cut) if d == 1 else (first + cut, count - cut)

    def part(yy, zz, c, first, count):
        return gathered.at[yy, zz, pl.ds((c * tiles + first) * 8, count * 8), :]

    def a1(c, d, h, arriving):
        zz = at_z(-d * (h if arriving else h - 1))
        span = halved(d, 0, tiles_a) if h == 4 else (0, tiles_a)
        k = (0 if d == 1 else 4) + h - 1
        return remote(part(y, zz, c, *span), s_a1.at[c, k], r_a1.at[c, k], col_of(y, at_z(d)))

    def a2(c, d, h, arriving):
        yy = at_y(-d * (h if arriving else h - 1))
        zz = pl.ds(*(halved(d, 0, NZ) if h == 2 else (0, NZ)))
        k = (0 if d == 1 else 2) + h - 1
        return remote(
            part(yy, zz, c, 0, tiles_a), s_a2.at[c, k], r_a2.at[c, k], col_of(at_y(d), z)
        )

    def b1(c, d, h, arriving):
        yy = at_y(-d * (h if arriving else h - 1))
        span = halved(d, tiles_a, tiles_b) if h == 2 else (tiles_a, tiles_b)
        k = (0 if d == 1 else 2) + h - 1
        return remote(part(yy, z, c, *span), s_b1.at[c, k], r_b1.at[c, k], col_of(at_y(d), z))

    def b2(c, d, h, arriving):
        zz = at_z(-d * (h if arriving else h - 1))
        yy = pl.ds(*(halved(d, 0, NY) if h == 4 else (0, NY)))
        k = (0 if d == 1 else 4) + h - 1
        return remote(
            part(yy, zz, c, tiles_a, tiles_b), s_b2.at[c, k], r_b2.at[c, k], col_of(y, at_z(d))
        )

    def begin(what, c):
        for d in (1, -1):
            what(c, d, 1, False).start()

    def forward(what, c, h):
        for d in (1, -1):
            what(c, d, h, True).wait_recv()
            what(c, d, h + 1, False).start()

    def arrive(what, c, h):
        for d in (1, -1):
            what(c, d, h, True).wait_recv()

    def sent(what, c, hops):
        for d in (1, -1):
            for h in range(1, hops + 1):
                what(c, d, h, False).wait_send()

    u_own_sib = remote(ug.at[row], s_u.at[0], r_u.at[0], {"row": sib})
    u_own_far = remote(ug.at[row], s_u.at[1], r_u.at[1], {"row": far})
    u_fwd = remote(ug.at[far], s_u.at[2], r_u.at[2], {"row": sib})
    far_sib = lax.rem(sib + 2, ROWS)

    def u_arrive(k, which):
        remote(ug.at[which], s_u.at[k], r_u.at[k], {"row": sib}).wait_recv()

    def exchange(c):
        return pltpu.make_async_remote_copy(
            src_ref=mine.at[c], dst_ref=rx_ref.at[c], send_sem=s_x.at[c], recv_sem=r_x.at[c],
            device_id={"layer": 1 - layer}, device_id_type=MESH,
        )

    def store_out(c):
        return pltpu.make_async_copy(mine.at[c], mine_ref.at[c], l_out.at[c])

    load_anc = pltpu.make_async_copy(anc_ref, anc, l_anc)
    load_anc.start()

    barrier = pltpu.get_barrier_semaphore()
    greeted = [
        {"row": sib}, {"row": far}, {"layer": 1 - layer},
        col_of(at_y(1), z), col_of(at_y(-1), z), col_of(y, at_z(1)), col_of(y, at_z(-1)),
    ]
    for other in greeted:
        pl.semaphore_signal(barrier, inc=1, device_id=other, device_id_type=MESH)

    for panel in range(PANELS):
        ug[row, panel * 128 : panel * 128 + 128, :] = up_ref[0, panel]
    ug[row, PANELS * 128 :, :] = fu_ref[...]

    for r in range(BLOCKS):
        lanes = slice(r * BLK, r * BLK + BLK)
        for q in range(TILES - 1):
            own[r * TILES + q] = low_ref[q, :, lanes]
        own[r * TILES + TILES - 1] = fl_ref[:, lanes]
    high[0] = jnp.zeros(high.shape[1:], BF16)
    low[0] = jnp.zeros(low.shape[1:], BF16)

    def place(c):
        for n in range(tiles):
            t = c * tiles + n
            gathered[y, z, pl.ds(t * 8, 8), :] = own[tab_ref[SOURCE + t // BLK, lax.rem(t, BLK)]]

    def unpack(c):
        for n in range(tiles):
            t = c * tiles + n
            piece = gathered[:, :, pl.ds(t * 8, 8), :].reshape(256, BLK)
            high[t + 1], low[t + 1] = split(piece)

    pl.semaphore_wait(barrier, len(greeted))

    u_own_far.start()
    u_own_sib.start()

    def scale(mask_ref, *index):
        return mask_ref[index].astype(F32)

    def prepare_upper():
        u_arrive(0, sib)
        u_arrive(1, far)
        u_fwd.start()
        u_arrive(2, far_sib)
        for half in range(2):
            cols = slice(half * BLK, half * BLK + BLK)
            for panel in range(PANELS):
                keep = scale(ub_ref, 0, panel, col * 2 + half)
                for odd in range(2):
                    for pair in range(NY * NZ // 2):
                        r, at = pair // 4, panel * 128 + pair % 4 * 32 + odd * 8
                        both = jnp.concatenate(
                            [ug[r, at : at + 8, cols], ug[r, at + 16 : at + 24, cols]], axis=0
                        )
                        above, below = split(both * keep)
                        to = slice(pair * 16, pair * 16 + 16)
                        uh[panel * 2 + odd, to, cols] = above
                        ul[panel * 2 + odd, to, cols] = below
            keep = scale(fub_ref, col * 2 + half)
            for r in range(ROWS):
                above, below = split(ug[r, PANELS * 128 :, cols] * keep)
                uh[TILES - 1, r * 64 : r * 64 + 64, cols] = above
                ul[TILES - 1, r * 64 : r * 64 + 64, cols] = below

    def compute(c, r):
        at = row * BLOCKS + c * R + r
        total = anc[tab_ref[ORDER, at]]
        for q in range(TILES):
            t = tab_ref[T_OF + q, at]
            total = total - contract(high[t], low[t], uh[q], ul[q])
        mine[c, r * BLK : r * BLK + BLK, :] = total

    def upper(c):
        @pl.when(c == 0)
        def _():
            load_anc.wait()
            prepare_upper()

    def work(c):
        unpack(c)
        for r in range(R):
            compute(c, r)
        exchange(c).start()
        store_out(c).start()

    def clear(c):
        sent(a1, c, 4)
        sent(b1, c, 2)
        sent(a2, c, 2)
        sent(b2, c, 4)

    def starts(what):
        return lambda c: begin(what, c)

    def moves(what, hop):
        return lambda c: forward(what, c, hop)

    def ends(what, hop):
        return lambda c: arrive(what, c, hop)

    def step(i, _):
        def run(offset, *actions):
            @pl.when((i >= offset) & (i < chunks + offset))
            def _():
                for action in actions:
                    action(i - offset)

        run(0, place, starts(a1), starts(b1))
        run(1, moves(a1, 1), moves(b1, 1))
        run(2, moves(a1, 2), ends(b1, 2), starts(b2))
        run(3, moves(a1, 3), moves(b2, 1))
        run(4, ends(a1, 4), starts(a2), moves(b2, 2))
        run(5, moves(a2, 1), moves(b2, 3))
        run(6, upper, ends(a2, 2), ends(b2, 4), work)
        run(7, clear)
        return 0

    lax.fori_loop(0, chunks + 8, step, 0)
    u_own_sib.wait_send()
    u_own_far.wait_send()
    u_fwd.wait_send()

    def drain(c, _):
        exchange(c).wait()
        store_out(c).wait()
        return 0

    lax.fori_loop(0, chunks, drain, 0)


def tables(lb_ref, flb_ref, tab_ref, mask, other, sent, came):
    layer = lax.axis_index("layer")
    row = lax.axis_index("row")
    barrier = pltpu.get_barrier_semaphore()
    target = {"layer": 1 - layer}
    pl.semaphore_signal(barrier, inc=1, device_id=target, device_id_type=MESH)
    mask[...] = jnp.zeros_like(mask)
    mask[0:PANELS, 0:64] = lb_ref[0].astype(F32)
    mask[PANELS : PANELS + 1, 0:64] = flb_ref[...].astype(F32)
    pl.semaphore_wait(barrier, 1)
    copy = pltpu.make_async_remote_copy(
        src_ref=mask, dst_ref=other, send_sem=sent, recv_sem=came,
        device_id=target, device_id_type=MESH,
    )
    copy.start()
    square = (BLK, BLK)
    sub = lax.broadcasted_iota(jnp.int32, square, 0)
    lane = lax.broadcasted_iota(jnp.int32, square, 1)
    same = ((sub >> 4) == (lane >> 4)).astype(F32)
    earlier = (sub < lane).astype(F32)

    def ranked(held):
        weight = 2.0 * jnp.sum(held[0:PANELS], axis=0, keepdims=True) + held[PANELS : PANELS + 1]
        here = jnp.broadcast_to(weight, square)
        there = here.T
        before = jnp.where(there < here, 1.0, jnp.where(there == here, earlier, 0.0)) * same
        place = jnp.sum(before, axis=0, keepdims=True)
        start = jnp.sum(before * there, axis=0, keepdims=True)
        most = jnp.max(jnp.sum(same * there, axis=0, keepdims=True), axis=1, keepdims=True)
        return place, start, most

    held = mask[...]
    place, start, most = ranked(held)
    has = [held[min(q // 2, PANELS) : min(q // 2, PANELS) + 1] for q in range(TILES)]
    spots = []
    for q in range(TILES):
        spots.append(start)
        start = start + has[q]
    ours = ((lax.broadcasted_iota(jnp.int32, (1, BLK), 1) >> 4) == row).astype(F32)
    rows = [h * ours * (spot + 1.0) - 1.0 for h, spot in zip(has, spots)] + [place]
    turned = jnp.concatenate(rows + [jnp.zeros((BLK - TILES - 1, BLK), F32)], axis=0).T
    lane_f = lane.astype(F32)
    within = (sub & 15).astype(F32)
    hit = jnp.where(turned[:, TILES : TILES + 1] == (lane & 15).astype(F32), same, 0.0)
    source = [jnp.zeros(square, F32) for _ in range(2)]
    for q in range(TILES):
        spot = turned[:, q : q + 1]
        code = within * float(TILES) + float(q)
        for part in range(2):
            source[part] = source[part] + jnp.where(spot == lane_f + float(part * BLK), code, 0.0)
    moved = [h * (spot + 1.0) for h, spot in zip(has, spots)]
    moved.append((lax.broadcasted_iota(jnp.int32, (1, BLK), 1) & 15).astype(F32))
    moved = jnp.concatenate(moved + [jnp.zeros((16 - len(moved), BLK), F32)], axis=0)
    moved = jnp.dot(moved, hit, precision=lax.Precision.HIGHEST, preferred_element_type=F32)
    out = [jnp.sum(value, axis=0, keepdims=True) for value in source]
    out.append(place)
    copy.wait()
    place_other, _, most_other = ranked(other[...])
    out.append(place_other)
    out.append(jnp.broadcast_to(jnp.maximum(most, most_other), (1, BLK)))
    tab_ref[0:TILES + 1, :] = (moved[0:TILES + 1] + 0.5).astype(jnp.int32)
    for n, value in enumerate(out):
        tab_ref[SOURCE + n : SOURCE + n + 1, :] = value.astype(jnp.int32)
    tab_ref[MOST + 1 :, :] = jnp.zeros((16 - MOST - 1, BLK), jnp.int32)


def combine(tab_ref, mine_ref, rx_ref, out_ref, mine, rx, total, sem_m, sem_r, sem_o):
    row = lax.axis_index("row")

    def loads(n):
        at = row * BLOCKS + n
        return (
            pltpu.make_async_copy(mine_ref.at[tab_ref[POS, at]], mine.at[n], sem_m.at[n]),
            pltpu.make_async_copy(rx_ref.at[tab_ref[POS_OTHER, at]], rx.at[n], sem_r.at[n]),
        )

    def store(n):
        return pltpu.make_async_copy(total.at[n], out_ref.at[n], sem_o.at[n])

    for n in range(BLOCKS):
        for load in loads(n):
            load.start()
    for n in range(BLOCKS):
        for load in loads(n):
            load.wait()
        total[n] = mine[n] + rx[n]
        store(n).start()
    for n in range(BLOCKS):
        store(n).wait()


VMEM = pl.BlockSpec(memory_space=pltpu.VMEM)
SMEM = pl.BlockSpec(memory_space=pltpu.SMEM)
HBM = pl.BlockSpec(memory_space=pl.ANY)


def gather_update(n, cols, rows):
    tiles, tiles_a = SIZES[n]
    dma = pltpu.SemaphoreType.DMA
    result = jax.ShapeDtypeStruct((CHUNKS, R * BLK, cols), F32)
    return pl.pallas_call(
        functools.partial(kernel, tiles, tiles_a),
        out_shape=(result, result),
        in_specs=[SMEM, HBM, VMEM, VMEM, SMEM, VMEM, VMEM, SMEM],
        out_specs=(HBM, HBM),
        scratch_shapes=[
            pltpu.VMEM((NY, NZ, CHUNKS * tiles * 8, BLK), F32),
            pltpu.VMEM((BLOCKS * TILES, 8, BLK), F32),
            pltpu.VMEM((CHUNKS * tiles + 1, 256, BLK), BF16),
            pltpu.VMEM((CHUNKS * tiles + 1, 256, BLK), BF16),
            pltpu.VMEM((ROWS, PANELS * 128 + 64, cols), F32),
            pltpu.VMEM((TILES, 256, cols), BF16),
            pltpu.VMEM((TILES, 256, cols), BF16),
            pltpu.VMEM((BLOCKS, BLK, cols), F32),
            pltpu.VMEM((CHUNKS, R * BLK, cols), F32),
            dma((CHUNKS, 8)), dma((CHUNKS, 8)),
            dma((CHUNKS, 4)), dma((CHUNKS, 4)),
            dma((CHUNKS, 4)), dma((CHUNKS, 4)),
            dma((CHUNKS, 8)), dma((CHUNKS, 8)),
            dma((3,)), dma((3,)),
            dma((CHUNKS,)), dma((CHUNKS,)),
            dma, dma((CHUNKS,)),
        ],
        compiler_params=pltpu.CompilerParams(
            collective_id=n + 1, has_side_effects=True, vmem_limit_bytes=56 << 20
        ),
        name="gather_update_exchange",
    )


def body(anc, low, up, lb, ub, fl, fu, flb, fub):
    rows, cols = anc.shape[1:]
    dma = pltpu.SemaphoreType.DMA
    tab = pl.pallas_call(
        tables,
        out_shape=jax.ShapeDtypeStruct((16, BLK), jnp.int32),
        in_specs=[VMEM, VMEM],
        out_specs=VMEM,
        scratch_shapes=[pltpu.VMEM((8, BLK), F32), pltpu.VMEM((8, BLK), F32), dma, dma],
        compiler_params=pltpu.CompilerParams(collective_id=0, has_side_effects=True),
        name="block_tables",
    )(lb, flb.reshape(1, -1))
    most = tab[MOST, 0]
    size = sum((most > tiles * CHUNKS).astype(jnp.int32) for tiles, _ in SIZES[:-1])
    mine, rx = lax.switch(
        size,
        [gather_update(n, cols, rows) for n in range(len(SIZES))],
        tab, anc.reshape(BLOCKS, BLK, cols), low.reshape(2 * PANELS, 8, rows), up, ub, fl, fu, fub,
    )
    blocks = (BLOCKS, BLK, cols)
    out = pl.pallas_call(
        combine,
        out_shape=jax.ShapeDtypeStruct(blocks, F32),
        in_specs=[SMEM, HBM, HBM],
        out_specs=HBM,
        scratch_shapes=[pltpu.VMEM(blocks, F32)] * 3 + [dma((BLOCKS,))] * 3,
        compiler_params=pltpu.CompilerParams(vmem_limit_bytes=16 << 20),
        name="layer_sum",
    )(tab, mine.reshape(blocks), rx.reshape(blocks))
    return out.reshape(rows, cols)


def solution(mesh):
    return jax.shard_map(
        body,
        mesh=mesh,
        in_specs=(
            P("layer", "row", "col"),
            P("layer", None, "col", "row"),
            P("layer", None, "row", "col"),
            P("layer", None, None),
            P("layer", None, None),
            P(("layer", "col"), "row"),
            P(("layer", "row"), "col"),
            P(),
            P(),
        ),
        out_specs=P("row", "col"),
        check_vma=False,
    )
```

```python
import functools

import jax
import jax.numpy as jnp
from jax import lax
from jax.experimental import pallas as pl
from jax.experimental.pallas import tpu as pltpu
from jax.sharding import PartitionSpec as P

BLK = 128
PANELS = 4
NY, NZ = 4, 8
ROWS = 4
R = 2
CHUNKS = 8
TILES = 9
BLOCKS = 16
SIZES = ((11, 7), (12, 7), (18, 11))
T_OF, ORDER, SOURCE, POS, POS_OTHER, MOST = 0, 9, 10, 12, 13, 14
MESH = pl.DeviceIdType.MESH
F32, BF16 = jnp.float32, jnp.bfloat16


def split(value):
    high = value.astype(BF16)
    return high, (value - high.astype(F32)).astype(BF16)


def contract(high, low, upper_high, upper_low):

    def dot(a, b):
        return lax.dot_general(a, b, (((0,), (0,)), ((), ())), preferred_element_type=F32)

    return dot(high, upper_high) + dot(high, upper_low) + dot(low, upper_high)


def kernel(
    tiles, tiles_a, tab_ref, anc_ref, low_ref, up_ref, ub_ref, fl_ref, fu_ref, fub_ref,
    mine_ref, rx_ref,
    gathered, own, high, low, ug, uh, ul, anc, mine,
    s_a1, r_a1, s_a2, r_a2, s_b1, r_b1, s_b2, r_b2, s_u, r_u, s_x, r_x, l_anc, l_out,
):
    chunks = CHUNKS
    tiles_b = tiles - tiles_a
    layer = lax.axis_index("layer")
    row = lax.axis_index("row")
    col = lax.axis_index("col")
    y, z = col // NZ, lax.rem(col, NZ)
    sib = row + 1 - 2 * lax.rem(row, 2)
    far = lax.rem(row + 2, ROWS)

    def at_y(d):
        return lax.rem(y + d + NY, NY)

    def at_z(d):
        return lax.rem(z + d + NZ, NZ)

    def col_of(yy, zz):
        return {"col": yy * NZ + zz}

    def remote(ref, ssem, rsem, target):
        return pltpu.make_async_remote_copy(
            src_ref=ref, dst_ref=ref, send_sem=ssem, recv_sem=rsem,
            device_id=target, device_id_type=MESH,
        )

    def halved(d, first, count):
        cut = count // 2
        return (first, cut) if d == 1 else (first + cut, count - cut)

    def part(yy, zz, c, first, count):
        return gathered.at[yy, zz, pl.ds((c * tiles + first) * 8, count * 8), :]

    def a1(c, d, h, arriving):
        zz = at_z(-d * (h if arriving else h - 1))
        span = halved(d, 0, tiles_a) if h == 4 else (0, tiles_a)
        k = (0 if d == 1 else 4) + h - 1
        return remote(part(y, zz, c, *span), s_a1.at[c, k], r_a1.at[c, k], col_of(y, at_z(d)))

    def line(c, d, far_z, arriving):
        yy = at_y(-d if arriving else 0)
        zz = at_z(far_z)
        k = (0 if d == 1 else NZ + 1) + far_z % NZ
        return remote(
            part(yy, zz, c, 0, tiles_a), s_a2.at[c, k], r_a2.at[c, k], col_of(at_y(d), z)
        )

    def onward(c, d, arriving):
        yy = at_y(-d * (2 if arriving else 1))
        zz = pl.ds(*halved(d, 0, NZ))
        k = (0 if d == 1 else NZ + 1) + NZ
        return remote(
            part(yy, zz, c, 0, tiles_a), s_a2.at[c, k], r_a2.at[c, k], col_of(at_y(d), z)
        )

    def spread(*far_z):
        def act(c):
            for k in far_z:
                for d in (1, -1):
                    line(c, d, k, False).start()

        return act

    def a2_on(c):
        for d in (1, -1):
            for k in range(NZ):
                line(c, d, k, True).wait_recv()
            onward(c, d, False).start()

    def a2_end(c):
        for d in (1, -1):
            onward(c, d, True).wait_recv()

    def a2_sent(c):
        for d in (1, -1):
            for k in range(NZ):
                line(c, d, k, False).wait_send()
            onward(c, d, False).wait_send()

    def b1(c, d, h, arriving):
        yy = at_y(-d * (h if arriving else h - 1))
        span = halved(d, tiles_a, tiles_b) if h == 2 else (tiles_a, tiles_b)
        k = (0 if d == 1 else 2) + h - 1
        return remote(part(yy, z, c, *span), s_b1.at[c, k], r_b1.at[c, k], col_of(at_y(d), z))

    def b2(c, d, h, arriving):
        zz = at_z(-d * (h if arriving else h - 1))
        yy = pl.ds(*(halved(d, 0, NY) if h == 4 else (0, NY)))
        k = (0 if d == 1 else 4) + h - 1
        return remote(
            part(yy, zz, c, tiles_a, tiles_b), s_b2.at[c, k], r_b2.at[c, k], col_of(y, at_z(d))
        )

    def begin(what, c):
        for d in (1, -1):
            what(c, d, 1, False).start()

    def forward(what, c, h):
        for d in (1, -1):
            what(c, d, h, True).wait_recv()
            what(c, d, h + 1, False).start()

    def arrive(what, c, h):
        for d in (1, -1):
            what(c, d, h, True).wait_recv()

    def sent(what, c, hops):
        for d in (1, -1):
            for h in range(1, hops + 1):
                what(c, d, h, False).wait_send()

    u_own_sib = remote(ug.at[row], s_u.at[0], r_u.at[0], {"row": sib})
    u_own_far = remote(ug.at[row], s_u.at[1], r_u.at[1], {"row": far})
    u_fwd = remote(ug.at[far], s_u.at[2], r_u.at[2], {"row": sib})
    far_sib = lax.rem(sib + 2, ROWS)

    def u_arrive(k, which):
        remote(ug.at[which], s_u.at[k], r_u.at[k], {"row": sib}).wait_recv()

    def exchange(c):
        return pltpu.make_async_remote_copy(
            src_ref=mine.at[c], dst_ref=rx_ref.at[c], send_sem=s_x.at[c], recv_sem=r_x.at[c],
            device_id={"layer": 1 - layer}, device_id_type=MESH,
        )

    def store_out(c):
        return pltpu.make_async_copy(mine.at[c], mine_ref.at[c], l_out.at[c])

    load_anc = pltpu.make_async_copy(anc_ref, anc, l_anc)
    load_anc.start()

    barrier = pltpu.get_barrier_semaphore()
    greeted = [
        {"row": sib}, {"row": far}, {"layer": 1 - layer},
        col_of(at_y(1), z), col_of(at_y(-1), z), col_of(y, at_z(1)), col_of(y, at_z(-1)),
    ]
    for other in greeted:
        pl.semaphore_signal(barrier, inc=1, device_id=other, device_id_type=MESH)

    for panel in range(PANELS):
        ug[row, panel * 128 : panel * 128 + 128, :] = up_ref[0, panel]
    ug[row, PANELS * 128 :, :] = fu_ref[...]

    for r in range(BLOCKS):
        lanes = slice(r * BLK, r * BLK + BLK)
        for q in range(TILES - 1):
            own[r * TILES + q] = low_ref[q, :, lanes]
        own[r * TILES + TILES - 1] = fl_ref[:, lanes]
    high[0] = jnp.zeros(high.shape[1:], BF16)
    low[0] = jnp.zeros(low.shape[1:], BF16)

    def place(c):
        for n in range(tiles):
            t = c * tiles + n
            gathered[y, z, pl.ds(t * 8, 8), :] = own[tab_ref[SOURCE + t // BLK, lax.rem(t, BLK)]]

    def unpack(c):
        for n in range(tiles):
            t = c * tiles + n
            piece = gathered[:, :, pl.ds(t * 8, 8), :].reshape(256, BLK)
            high[t + 1], low[t + 1] = split(piece)

    pl.semaphore_wait(barrier, len(greeted))

    u_own_far.start()
    u_own_sib.start()

    def scale(mask_ref, *index):
        return mask_ref[index].astype(F32)

    def convert_upper(r):
        for half in range(2):
            cols = slice(half * BLK, half * BLK + BLK)
            for panel in range(PANELS):
                keep = scale(ub_ref, 0, panel, col * 2 + half)
                for odd in range(2):
                    for pair in range(4):
                        at = panel * 128 + pair * 32 + odd * 8
                        both = jnp.concatenate(
                            [ug[r, at : at + 8, cols], ug[r, at + 16 : at + 24, cols]], axis=0
                        )
                        above, below = split(both * keep)
                        to = pl.ds(pl.multiple_of(r * 64 + pair * 16, 16), 16)
                        uh[panel * 2 + odd, to, cols] = above
                        ul[panel * 2 + odd, to, cols] = below
            keep = scale(fub_ref, col * 2 + half)
            above, below = split(ug[r, PANELS * 128 :, cols] * keep)
            to = pl.ds(pl.multiple_of(r * 64, 64), 64)
            uh[TILES - 1, to, cols] = above
            ul[TILES - 1, to, cols] = below

    def compute(c, r):
        at = row * BLOCKS + c * R + r
        total = anc[tab_ref[ORDER, at]]
        for q in range(TILES):
            t = tab_ref[T_OF + q, at]
            total = total - contract(high[t], low[t], uh[q], ul[q])
        mine[c * R + r] = total

    def upper_near(c):
        @pl.when(c == 0)
        def _():
            load_anc.wait()
            convert_upper(row)
            u_arrive(0, sib)
            convert_upper(sib)

    def upper_far(c):
        @pl.when(c == 0)
        def _():
            u_arrive(1, far)
            u_fwd.start()
            convert_upper(far)

    def upper_last(c):
        @pl.when(c == 0)
        def _():
            u_arrive(2, far_sib)
            convert_upper(far_sib)

    def work(c):
        unpack(c)
        for r in range(R):
            compute(c, r)
            exchange(c * R + r).start()
            store_out(c * R + r).start()

    def clear(c):
        sent(a1, c, 4)
        sent(b1, c, 2)
        a2_sent(c)
        sent(b2, c, 4)

    def starts(what):
        return lambda c: begin(what, c)

    def moves(what, hop):
        return lambda c: forward(what, c, hop)

    def ends(what, hop):
        return lambda c: arrive(what, c, hop)

    def step(i, _):
        def run(offset, *actions):
            @pl.when((i >= offset) & (i < chunks + offset))
            def _():
                for action in actions:
                    action(i - offset)

        run(0, place, starts(a1), starts(b1), spread(0))
        run(1, moves(a1, 1), moves(b1, 1), spread(1, -1))
        run(2, moves(a1, 2), ends(b1, 2), starts(b2), spread(2, -2))
        run(2, upper_near)
        run(3, moves(a1, 3), moves(b2, 1), spread(3, -3))
        run(4, ends(a1, 4), spread(4), moves(b2, 2))
        run(4, upper_far)
        run(5, a2_on, moves(b2, 3))
        run(6, upper_last, a2_end, ends(b2, 4), work)
        run(7, clear)
        return 0

    lax.fori_loop(0, chunks + 8, step, 0)
    u_own_sib.wait_send()
    u_own_far.wait_send()
    u_fwd.wait_send()

    def drain(c, _):
        exchange(c).wait()
        store_out(c).wait()
        return 0

    lax.fori_loop(0, BLOCKS, drain, 0)


def tables(lb_ref, flb_ref, tab_ref, mask, other, sent, came):
    layer = lax.axis_index("layer")
    row = lax.axis_index("row")
    barrier = pltpu.get_barrier_semaphore()
    target = {"layer": 1 - layer}
    pl.semaphore_signal(barrier, inc=1, device_id=target, device_id_type=MESH)
    mask[...] = jnp.zeros_like(mask)
    mask[0:PANELS, 0:64] = lb_ref[0].astype(F32)
    mask[PANELS : PANELS + 1, 0:64] = flb_ref[...].astype(F32)
    pl.semaphore_wait(barrier, 1)
    copy = pltpu.make_async_remote_copy(
        src_ref=mask, dst_ref=other, send_sem=sent, recv_sem=came,
        device_id=target, device_id_type=MESH,
    )
    copy.start()
    square = (BLK, BLK)
    sub = lax.broadcasted_iota(jnp.int32, square, 0)
    lane = lax.broadcasted_iota(jnp.int32, square, 1)
    same = ((sub >> 4) == (lane >> 4)).astype(F32)
    earlier = (sub < lane).astype(F32)

    def ranked(held):
        weight = 2.0 * jnp.sum(held[0:PANELS], axis=0, keepdims=True) + held[PANELS : PANELS + 1]
        here = jnp.broadcast_to(weight, square)
        there = here.T
        before = jnp.where(there < here, 1.0, jnp.where(there == here, earlier, 0.0)) * same
        place = jnp.sum(before, axis=0, keepdims=True)
        start = jnp.sum(before * there, axis=0, keepdims=True)
        most = jnp.max(jnp.sum(same * there, axis=0, keepdims=True), axis=1, keepdims=True)
        return place, start, most

    held = mask[...]
    place, start, most = ranked(held)
    has = [held[min(q // 2, PANELS) : min(q // 2, PANELS) + 1] for q in range(TILES)]
    spots = []
    for q in range(TILES):
        spots.append(start)
        start = start + has[q]
    ours = ((lax.broadcasted_iota(jnp.int32, (1, BLK), 1) >> 4) == row).astype(F32)
    rows = [h * ours * (spot + 1.0) - 1.0 for h, spot in zip(has, spots)] + [place]
    turned = jnp.concatenate(rows + [jnp.zeros((BLK - TILES - 1, BLK), F32)], axis=0).T
    lane_f = lane.astype(F32)
    within = (sub & 15).astype(F32)
    hit = jnp.where(turned[:, TILES : TILES + 1] == (lane & 15).astype(F32), same, 0.0)
    source = [jnp.zeros(square, F32) for _ in range(2)]
    for q in range(TILES):
        spot = turned[:, q : q + 1]
        code = within * float(TILES) + float(q)
        for part in range(2):
            source[part] = source[part] + jnp.where(spot == lane_f + float(part * BLK), code, 0.0)
    moved = [h * (spot + 1.0) for h, spot in zip(has, spots)]
    moved.append((lax.broadcasted_iota(jnp.int32, (1, BLK), 1) & 15).astype(F32))
    moved = jnp.concatenate(moved + [jnp.zeros((16 - len(moved), BLK), F32)], axis=0)
    moved = jnp.dot(moved, hit, precision=lax.Precision.HIGHEST, preferred_element_type=F32)
    out = [jnp.sum(value, axis=0, keepdims=True) for value in source]
    out.append(place)
    copy.wait()
    place_other, _, most_other = ranked(other[...])
    out.append(place_other)
    out.append(jnp.broadcast_to(jnp.maximum(most, most_other), (1, BLK)))
    tab_ref[0:TILES + 1, :] = (moved[0:TILES + 1] + 0.5).astype(jnp.int32)
    for n, value in enumerate(out):
        tab_ref[SOURCE + n : SOURCE + n + 1, :] = value.astype(jnp.int32)
    tab_ref[MOST + 1 :, :] = jnp.zeros((16 - MOST - 1, BLK), jnp.int32)


def combine(tab_ref, mine_ref, rx_ref, out_ref, total, sem_o):
    row = lax.axis_index("row")

    def store(n):
        return pltpu.make_async_copy(total.at[n], out_ref.at[n], sem_o.at[n])

    for n in range(BLOCKS):
        at = row * BLOCKS + n
        total[n] = mine_ref[tab_ref[POS, at]] + rx_ref[tab_ref[POS_OTHER, at]]
        store(n).start()
    for n in range(BLOCKS):
        store(n).wait()


VMEM = pl.BlockSpec(memory_space=pltpu.VMEM)
SMEM = pl.BlockSpec(memory_space=pltpu.SMEM)
HBM = pl.BlockSpec(memory_space=pl.ANY)


def gather_update(n, cols, rows):
    tiles, tiles_a = SIZES[n]
    dma = pltpu.SemaphoreType.DMA
    result = jax.ShapeDtypeStruct((BLOCKS, BLK, cols), F32)
    return pl.pallas_call(
        functools.partial(kernel, tiles, tiles_a),
        out_shape=(result, result),
        in_specs=[SMEM, HBM, VMEM, VMEM, SMEM, VMEM, VMEM, SMEM],
        out_specs=(HBM, HBM),
        scratch_shapes=[
            pltpu.VMEM((NY, NZ, CHUNKS * tiles * 8, BLK), F32),
            pltpu.VMEM((BLOCKS * TILES, 8, BLK), F32),
            pltpu.VMEM((CHUNKS * tiles + 1, 256, BLK), BF16),
            pltpu.VMEM((CHUNKS * tiles + 1, 256, BLK), BF16),
            pltpu.VMEM((ROWS, PANELS * 128 + 64, cols), F32),
            pltpu.VMEM((TILES, 256, cols), BF16),
            pltpu.VMEM((TILES, 256, cols), BF16),
            pltpu.VMEM((BLOCKS, BLK, cols), F32),
            pltpu.VMEM((BLOCKS, BLK, cols), F32),
            dma((CHUNKS, 8)), dma((CHUNKS, 8)),
            dma((CHUNKS, 18)), dma((CHUNKS, 18)),
            dma((CHUNKS, 4)), dma((CHUNKS, 4)),
            dma((CHUNKS, 8)), dma((CHUNKS, 8)),
            dma((3,)), dma((3,)),
            dma((BLOCKS,)), dma((BLOCKS,)),
            dma, dma((BLOCKS,)),
        ],
        compiler_params=pltpu.CompilerParams(
            collective_id=n + 1, has_side_effects=True, vmem_limit_bytes=56 << 20
        ),
        name="gather_update_exchange",
    )


def body(anc, low, up, lb, ub, fl, fu, flb, fub):
    rows, cols = anc.shape[1:]
    dma = pltpu.SemaphoreType.DMA
    tab = pl.pallas_call(
        tables,
        out_shape=jax.ShapeDtypeStruct((16, BLK), jnp.int32),
        in_specs=[VMEM, VMEM],
        out_specs=VMEM,
        scratch_shapes=[pltpu.VMEM((8, BLK), F32), pltpu.VMEM((8, BLK), F32), dma, dma],
        compiler_params=pltpu.CompilerParams(collective_id=0, has_side_effects=True),
        name="block_tables",
    )(lb, flb.reshape(1, -1))
    most = tab[MOST, 0]
    size = sum((most > tiles * CHUNKS).astype(jnp.int32) for tiles, _ in SIZES[:-1])
    mine, rx = lax.switch(
        size,
        [gather_update(n, cols, rows) for n in range(len(SIZES))],
        tab, anc.reshape(BLOCKS, BLK, cols), low.reshape(2 * PANELS, 8, rows), up, ub, fl, fu, fub,
    )
    blocks = (BLOCKS, BLK, cols)
    out = pl.pallas_call(
        combine,
        out_shape=jax.ShapeDtypeStruct(blocks, F32),
        in_specs=[SMEM, VMEM, VMEM],
        out_specs=HBM,
        scratch_shapes=[pltpu.VMEM(blocks, F32), dma((BLOCKS,))],
        compiler_params=pltpu.CompilerParams(vmem_limit_bytes=16 << 20),
        name="layer_sum",
    )(tab, mine, rx)
    return out.reshape(rows, cols)


def solution(mesh):
    return jax.shard_map(
        body,
        mesh=mesh,
        in_specs=(
            P("layer", "row", "col"),
            P("layer", None, "col", "row"),
            P("layer", None, "row", "col"),
            P("layer", None, None),
            P("layer", None, None),
            P(("layer", "col"), "row"),
            P(("layer", "row"), "col"),
            P(),
            P(),
        ),
        out_specs=P("row", "col"),
        check_vma=False,
    )
```

```python
import functools

import jax
import jax.numpy as jnp
from jax import lax
from jax.experimental import pallas as pl
from jax.experimental.pallas import tpu as pltpu
from jax.sharding import PartitionSpec as P

BLK = 128
PANELS = 4
NY, NZ = 4, 8
ROWS = 4
R = 2
CHUNKS = 8
TILES = 9
BLOCKS = 16
SIZES = ((10, 6), (11, 7), (12, 7), (18, 11))
T_OF, ORDER, SOURCE, POS, POS_OTHER = 0, 9, 10, 12, 13
MESH = pl.DeviceIdType.MESH
F32, BF16 = jnp.float32, jnp.bfloat16


def split(value):
    high = value.astype(BF16)
    return high, (value - high.astype(F32)).astype(BF16)


def contract(high, low, upper, q):
    cols = upper.shape[2] // 2

    def dot(a, b):
        return lax.dot_general(a, b, (((0,), (0,)), ((), ())), preferred_element_type=F32)

    both = dot(high, upper[q])
    return both[:, :cols] + both[:, cols:] + dot(low, upper[q, :, :cols])


def kernel(
    tiles, tiles_a, tab_ref, anc_ref, low_ref, up_ref, ub_ref, fl_ref, fu_ref, fub_ref,
    mine_ref, rx_ref,
    gathered, own, high, low, ug, upper, anc, mine,
    s_a1, r_a1, s_a2, r_a2, s_b1, r_b1, s_b2, r_b2, s_u, r_u, s_x, r_x, l_anc, l_out,
):
    chunks = CHUNKS
    tiles_b = tiles - tiles_a
    layer = lax.axis_index("layer")
    row = lax.axis_index("row")
    col = lax.axis_index("col")
    y, z = col // NZ, lax.rem(col, NZ)
    sib = row + 1 - 2 * lax.rem(row, 2)
    far = lax.rem(row + 2, ROWS)

    def at_y(d):
        return lax.rem(y + d + NY, NY)

    def at_z(d):
        return lax.rem(z + d + NZ, NZ)

    def col_of(yy, zz):
        return {"col": yy * NZ + zz}

    def remote(ref, ssem, rsem, target):
        return pltpu.make_async_remote_copy(
            src_ref=ref, dst_ref=ref, send_sem=ssem, recv_sem=rsem,
            device_id=target, device_id_type=MESH,
        )

    def halved(d, first, count):
        cut = count // 2
        return (first, cut) if d == 1 else (first + cut, count - cut)

    def part(yy, zz, c, first, count):
        return gathered.at[yy, zz, pl.ds((c * tiles + first) * 8, count * 8), :]

    def a1(c, d, h, arriving):
        zz = at_z(-d * (h if arriving else h - 1))
        span = halved(d, 0, tiles_a) if h == 4 else (0, tiles_a)
        k = (0 if d == 1 else 4) + h - 1
        return remote(part(y, zz, c, *span), s_a1.at[c, k], r_a1.at[c, k], col_of(y, at_z(d)))

    def line(c, d, far_z, arriving):
        yy = at_y(-d if arriving else 0)
        zz = at_z(far_z)
        k = (0 if d == 1 else NZ + 1) + far_z % NZ
        return remote(
            part(yy, zz, c, 0, tiles_a), s_a2.at[c, k], r_a2.at[c, k], col_of(at_y(d), z)
        )

    def onward(c, d, arriving):
        yy = at_y(-d * (2 if arriving else 1))
        zz = pl.ds(*halved(d, 0, NZ))
        k = (0 if d == 1 else NZ + 1) + NZ
        return remote(
            part(yy, zz, c, 0, tiles_a), s_a2.at[c, k], r_a2.at[c, k], col_of(at_y(d), z)
        )

    def spread(*far_z):
        def act(c):
            for k in far_z:
                for d in (1, -1):
                    line(c, d, k, False).start()

        return act

    def a2_on(c):
        for d in (1, -1):
            for k in range(NZ):
                line(c, d, k, True).wait_recv()
            onward(c, d, False).start()

    def a2_end(c):
        for d in (1, -1):
            onward(c, d, True).wait_recv()

    def a2_sent(c):
        for d in (1, -1):
            for k in range(NZ):
                line(c, d, k, False).wait_send()
            onward(c, d, False).wait_send()

    def b1(c, d, h, arriving):
        yy = at_y(-d * (h if arriving else h - 1))
        span = halved(d, tiles_a, tiles_b) if h == 2 else (tiles_a, tiles_b)
        k = (0 if d == 1 else 2) + h - 1
        return remote(part(yy, z, c, *span), s_b1.at[c, k], r_b1.at[c, k], col_of(at_y(d), z))

    def b2(c, d, h, arriving):
        zz = at_z(-d * (h if arriving else h - 1))
        yy = pl.ds(*(halved(d, 0, NY) if h == 4 else (0, NY)))
        k = (0 if d == 1 else 4) + h - 1
        return remote(
            part(yy, zz, c, tiles_a, tiles_b), s_b2.at[c, k], r_b2.at[c, k], col_of(y, at_z(d))
        )

    def begin(what, c):
        for d in (1, -1):
            what(c, d, 1, False).start()

    def forward(what, c, h):
        for d in (1, -1):
            what(c, d, h, True).wait_recv()
            what(c, d, h + 1, False).start()

    def arrive(what, c, h):
        for d in (1, -1):
            what(c, d, h, True).wait_recv()

    def sent(what, c, hops):
        for d in (1, -1):
            for h in range(1, hops + 1):
                what(c, d, h, False).wait_send()

    u_own_sib = remote(ug.at[row], s_u.at[0], r_u.at[0], {"row": sib})
    u_own_far = remote(ug.at[row], s_u.at[1], r_u.at[1], {"row": far})
    u_fwd = remote(ug.at[far], s_u.at[2], r_u.at[2], {"row": sib})
    far_sib = lax.rem(sib + 2, ROWS)

    def u_arrive(k, which):
        remote(ug.at[which], s_u.at[k], r_u.at[k], {"row": sib}).wait_recv()

    def exchange(c):
        return pltpu.make_async_remote_copy(
            src_ref=mine.at[c], dst_ref=rx_ref.at[c], send_sem=s_x.at[c], recv_sem=r_x.at[c],
            device_id={"layer": 1 - layer}, device_id_type=MESH,
        )

    def store_out(c):
        return pltpu.make_async_copy(mine.at[c], mine_ref.at[c], l_out.at[c])

    load_anc = pltpu.make_async_copy(anc_ref, anc, l_anc)
    load_anc.start()

    barrier = pltpu.get_barrier_semaphore()
    greeted = [
        {"row": sib}, {"row": far}, {"layer": 1 - layer},
        col_of(at_y(1), z), col_of(at_y(-1), z), col_of(y, at_z(1)), col_of(y, at_z(-1)),
    ]
    for other in greeted:
        pl.semaphore_signal(barrier, inc=1, device_id=other, device_id_type=MESH)

    for panel in range(PANELS):
        ug[row, panel * 128 : panel * 128 + 128, :] = up_ref[0, panel]
    ug[row, PANELS * 128 :, :] = fu_ref[...]

    for r in range(BLOCKS):
        lanes = slice(r * BLK, r * BLK + BLK)
        for q in range(TILES - 1):
            own[r * TILES + q] = low_ref[q, :, lanes]
        own[r * TILES + TILES - 1] = fl_ref[:, lanes]
    high[0] = jnp.zeros(high.shape[1:], BF16)
    low[0] = jnp.zeros(low.shape[1:], BF16)

    def place(c):
        for n in range(tiles):
            t = c * tiles + n
            gathered[y, z, pl.ds(t * 8, 8), :] = own[tab_ref[SOURCE + t // BLK, lax.rem(t, BLK)]]

    def unpack(c):
        for n in range(tiles):
            t = c * tiles + n
            piece = gathered[:, :, pl.ds(t * 8, 8), :].reshape(256, BLK)
            high[t + 1], low[t + 1] = split(piece)

    pl.semaphore_wait(barrier, len(greeted))

    u_own_far.start()
    u_own_sib.start()

    def scale(mask_ref, *index):
        return mask_ref[index].astype(F32)

    def convert_upper(r):
        for half in range(2):
            cols = slice(half * BLK, half * BLK + BLK)
            beside = slice((2 + half) * BLK, (3 + half) * BLK)
            for panel in range(PANELS):
                keep = scale(ub_ref, 0, panel, col * 2 + half)
                for odd in range(2):
                    for pair in range(4):
                        at = panel * 128 + pair * 32 + odd * 8
                        both = jnp.concatenate(
                            [ug[r, at : at + 8, cols], ug[r, at + 16 : at + 24, cols]], axis=0
                        )
                        above, below = split(both * keep)
                        to = pl.ds(pl.multiple_of(r * 64 + pair * 16, 16), 16)
                        upper[panel * 2 + odd, to, cols] = above
                        upper[panel * 2 + odd, to, beside] = below
            keep = scale(fub_ref, col * 2 + half)
            above, below = split(ug[r, PANELS * 128 :, cols] * keep)
            to = pl.ds(pl.multiple_of(r * 64, 64), 64)
            upper[TILES - 1, to, cols] = above
            upper[TILES - 1, to, beside] = below

    def compute(c, r):
        at = row * BLOCKS + c * R + r
        total = anc[tab_ref[ORDER, at]]
        for q in range(TILES):
            t = tab_ref[T_OF + q, at]
            total = total - contract(high[t], low[t], upper, q)
        mine[c * R + r] = total

    def upper_near(c):
        @pl.when(c == 0)
        def _():
            load_anc.wait()
            convert_upper(row)
            u_arrive(0, sib)
            convert_upper(sib)

    def upper_far(c):
        @pl.when(c == 0)
        def _():
            u_arrive(1, far)
            u_fwd.start()
            convert_upper(far)

    def upper_last(c):
        @pl.when(c == 0)
        def _():
            u_arrive(2, far_sib)
            convert_upper(far_sib)

    def work(c):
        unpack(c)
        for r in range(R):
            compute(c, r)
            exchange(c * R + r).start()
            store_out(c * R + r).start()

    def clear(c):
        sent(a1, c, 4)
        sent(b1, c, 2)
        a2_sent(c)
        sent(b2, c, 4)

    def starts(what):
        return lambda c: begin(what, c)

    def moves(what, hop):
        return lambda c: forward(what, c, hop)

    def ends(what, hop):
        return lambda c: arrive(what, c, hop)

    def step(i, _):
        def run(offset, *actions):
            @pl.when((i >= offset) & (i < chunks + offset))
            def _():
                for action in actions:
                    action(i - offset)

        run(0, place, starts(a1), starts(b1), spread(0))
        run(1, moves(a1, 1), moves(b1, 1), spread(1, -1))
        run(2, moves(a1, 2), ends(b1, 2), starts(b2), spread(2, -2))
        run(2, upper_near)
        run(3, moves(a1, 3), moves(b2, 1), spread(3, -3))
        run(4, ends(a1, 4), spread(4), moves(b2, 2))
        run(4, upper_far)
        run(5, a2_on, moves(b2, 3))
        run(6, upper_last, a2_end, ends(b2, 4), work)
        run(7, clear)
        return 0

    lax.fori_loop(0, chunks + 8, step, 0)
    u_own_sib.wait_send()
    u_own_far.wait_send()
    u_fwd.wait_send()

    def drain(c, _):
        exchange(c).wait()
        store_out(c).wait()
        return 0

    lax.fori_loop(0, BLOCKS, drain, 0)


def tables(lb_ref, flb_ref, tab_ref, size_ref, mask, other, sent, came):
    layer = lax.axis_index("layer")
    row = lax.axis_index("row")
    barrier = pltpu.get_barrier_semaphore()
    target = {"layer": 1 - layer}
    pl.semaphore_signal(barrier, inc=1, device_id=target, device_id_type=MESH)
    mask[...] = jnp.zeros_like(mask)
    mask[0:PANELS, 0:64] = lb_ref[0].astype(F32)
    mask[PANELS : PANELS + 1, 0:64] = flb_ref[...].astype(F32)
    pl.semaphore_wait(barrier, 1)
    copy = pltpu.make_async_remote_copy(
        src_ref=mask, dst_ref=other, send_sem=sent, recv_sem=came,
        device_id=target, device_id_type=MESH,
    )
    copy.start()
    square = (BLK, BLK)
    sub = lax.broadcasted_iota(jnp.int32, square, 0)
    lane = lax.broadcasted_iota(jnp.int32, square, 1)
    same = ((sub >> 4) == (lane >> 4)).astype(F32)
    earlier = (sub < lane).astype(F32)

    def ranked(held):
        weight = 2.0 * jnp.sum(held[0:PANELS], axis=0, keepdims=True) + held[PANELS : PANELS + 1]
        here = jnp.broadcast_to(weight, square)
        there = here.T
        before = jnp.where(there < here, 1.0, jnp.where(there == here, earlier, 0.0)) * same
        place = jnp.sum(before, axis=0, keepdims=True)
        start = jnp.sum(before * there, axis=0, keepdims=True)
        most = jnp.max(jnp.sum(same * there, axis=0, keepdims=True), axis=1, keepdims=True)
        return place, start, most

    held = mask[...]
    place, start, most = ranked(held)
    has = [held[min(q // 2, PANELS) : min(q // 2, PANELS) + 1] for q in range(TILES)]
    spots = []
    for q in range(TILES):
        spots.append(start)
        start = start + has[q]
    ours = ((lax.broadcasted_iota(jnp.int32, (1, BLK), 1) >> 4) == row).astype(F32)
    rows = [h * ours * (spot + 1.0) - 1.0 for h, spot in zip(has, spots)] + [place]
    turned = jnp.concatenate(rows + [jnp.zeros((BLK - TILES - 1, BLK), F32)], axis=0).T
    lane_f = lane.astype(F32)
    within = (sub & 15).astype(F32)
    hit = jnp.where(turned[:, TILES : TILES + 1] == (lane & 15).astype(F32), same, 0.0)
    source = [jnp.zeros(square, F32) for _ in range(2)]
    for q in range(TILES):
        spot = turned[:, q : q + 1]
        code = within * float(TILES) + float(q)
        for part in range(2):
            source[part] = source[part] + jnp.where(spot == lane_f + float(part * BLK), code, 0.0)
    moved = [h * (spot + 1.0) for h, spot in zip(has, spots)]
    moved.append((lax.broadcasted_iota(jnp.int32, (1, BLK), 1) & 15).astype(F32))
    moved = jnp.concatenate(moved + [jnp.zeros((16 - len(moved), BLK), F32)], axis=0)
    moved = jnp.dot(moved, hit, precision=lax.Precision.HIGHEST, preferred_element_type=F32)
    out = [jnp.sum(value, axis=0, keepdims=True) for value in source]
    out.append(place)
    copy.wait()
    place_other, _, most_other = ranked(other[...])
    out.append(place_other)
    most = jnp.max(jnp.maximum(most, most_other)).astype(jnp.int32)
    size = jnp.int32(0)
    for tiles, _ in SIZES[:-1]:
        size = size + (most > tiles * CHUNKS).astype(jnp.int32)
    size_ref[0] = size
    tab_ref[0:TILES + 1, :] = (moved[0:TILES + 1] + 0.5).astype(jnp.int32)
    for n, value in enumerate(out):
        tab_ref[SOURCE + n : SOURCE + n + 1, :] = value.astype(jnp.int32)
    tab_ref[POS_OTHER + 1 :, :] = jnp.zeros((15 - POS_OTHER, BLK), jnp.int32)


def combine(tab_ref, mine_ref, rx_ref, out_ref, total, sem_o):
    row = lax.axis_index("row")

    def store(n):
        return pltpu.make_async_copy(total.at[n], out_ref.at[n], sem_o.at[n])

    for n in range(BLOCKS):
        at = row * BLOCKS + n
        total[n] = mine_ref[tab_ref[POS, at]] + rx_ref[tab_ref[POS_OTHER, at]]
        store(n).start()
    for n in range(BLOCKS):
        store(n).wait()


VMEM = pl.BlockSpec(memory_space=pltpu.VMEM)
SMEM = pl.BlockSpec(memory_space=pltpu.SMEM)
HBM = pl.BlockSpec(memory_space=pl.ANY)


def gather_update(n, cols, rows):
    tiles, tiles_a = SIZES[n]
    dma = pltpu.SemaphoreType.DMA
    result = jax.ShapeDtypeStruct((BLOCKS, BLK, cols), F32)
    return pl.pallas_call(
        functools.partial(kernel, tiles, tiles_a),
        out_shape=(result, result),
        in_specs=[SMEM, HBM, VMEM, VMEM, SMEM, VMEM, VMEM, SMEM],
        out_specs=(HBM, HBM),
        scratch_shapes=[
            pltpu.VMEM((NY, NZ, CHUNKS * tiles * 8, BLK), F32),
            pltpu.VMEM((BLOCKS * TILES, 8, BLK), F32),
            pltpu.VMEM((CHUNKS * tiles + 1, 256, BLK), BF16),
            pltpu.VMEM((CHUNKS * tiles + 1, 256, BLK), BF16),
            pltpu.VMEM((ROWS, PANELS * 128 + 64, cols), F32),
            pltpu.VMEM((TILES, 256, 2 * cols), BF16),
            pltpu.VMEM((BLOCKS, BLK, cols), F32),
            pltpu.VMEM((BLOCKS, BLK, cols), F32),
            dma((CHUNKS, 8)), dma((CHUNKS, 8)),
            dma((CHUNKS, 18)), dma((CHUNKS, 18)),
            dma((CHUNKS, 4)), dma((CHUNKS, 4)),
            dma((CHUNKS, 8)), dma((CHUNKS, 8)),
            dma((3,)), dma((3,)),
            dma((BLOCKS,)), dma((BLOCKS,)),
            dma, dma((BLOCKS,)),
        ],
        compiler_params=pltpu.CompilerParams(
            collective_id=n + 1, has_side_effects=True, vmem_limit_bytes=56 << 20
        ),
        name="gather_update_exchange",
    )


def body(anc, low, up, lb, ub, fl, fu, flb, fub):
    rows, cols = anc.shape[1:]
    dma = pltpu.SemaphoreType.DMA
    tab, size = pl.pallas_call(
        tables,
        out_shape=(
            jax.ShapeDtypeStruct((16, BLK), jnp.int32), jax.ShapeDtypeStruct((1,), jnp.int32)
        ),
        in_specs=[VMEM, VMEM],
        out_specs=(VMEM, SMEM),
        scratch_shapes=[pltpu.VMEM((8, BLK), F32), pltpu.VMEM((8, BLK), F32), dma, dma],
        compiler_params=pltpu.CompilerParams(collective_id=0, has_side_effects=True),
        name="block_tables",
    )(lb, flb.reshape(1, -1))
    mine, rx = lax.switch(
        size[0],
        [gather_update(n, cols, rows) for n in range(len(SIZES))],
        tab, anc.reshape(BLOCKS, BLK, cols), low.reshape(2 * PANELS, 8, rows), up, ub, fl, fu, fub,
    )
    blocks = (BLOCKS, BLK, cols)
    out = pl.pallas_call(
        combine,
        out_shape=jax.ShapeDtypeStruct(blocks, F32),
        in_specs=[SMEM, VMEM, VMEM],
        out_specs=HBM,
        scratch_shapes=[pltpu.VMEM(blocks, F32), dma((BLOCKS,))],
        compiler_params=pltpu.CompilerParams(vmem_limit_bytes=16 << 20),
        name="layer_sum",
    )(tab, mine, rx)
    return out.reshape(rows, cols)


def solution(mesh):
    return jax.shard_map(
        body,
        mesh=mesh,
        in_specs=(
            P("layer", "row", "col"),
            P("layer", None, "col", "row"),
            P("layer", None, "row", "col"),
            P("layer", None, None),
            P("layer", None, None),
            P(("layer", "col"), "row"),
            P(("layer", "row"), "col"),
            P(),
            P(),
        ),
        out_specs=P("row", "col"),
        check_vma=False,
    )
```

```python
import functools

import jax
import jax.numpy as jnp
from jax import lax
from jax.experimental import pallas as pl
from jax.experimental.pallas import tpu as pltpu
from jax.sharding import PartitionSpec as P

BLK = 128
PANELS = 4
NY, NZ = 4, 8
ROWS = 4
R = 2
CHUNKS = 8
TILES = 9
BLOCKS = 16
SIZES = ((10, 6), (11, 7), (12, 7), (14, 8), (18, 11))
T_OF, ORDER, SOURCE, POS, POS_OTHER = 0, 9, 10, 12, 13
MESH = pl.DeviceIdType.MESH
F32, BF16 = jnp.float32, jnp.bfloat16


def split(value):
    high = value.astype(BF16)
    return high, (value - high.astype(F32)).astype(BF16)


def contract(high, low, upper, q):
    cols = upper.shape[2] // 2

    def dot(a, b):
        return lax.dot_general(a, b, (((0,), (0,)), ((), ())), preferred_element_type=F32)

    both = dot(high, upper[q])
    return both[:, :cols] + both[:, cols:] + dot(low, upper[q, :, :cols])


def kernel(
    tiles, tiles_a, tab_ref, anc_ref, low_ref, up_ref, ub_ref, fl_ref, fu_ref, fub_ref,
    mine_ref, rx_ref,
    gathered, own, high, low, ug, upper, anc, mine,
    s_a1, r_a1, s_a2, r_a2, s_b1, r_b1, s_b2, r_b2, s_u, r_u, s_x, r_x, l_anc, l_out,
):
    chunks = CHUNKS
    tiles_b = tiles - tiles_a
    layer = lax.axis_index("layer")
    row = lax.axis_index("row")
    col = lax.axis_index("col")
    y, z = col // NZ, lax.rem(col, NZ)
    sib = row + 1 - 2 * lax.rem(row, 2)
    far = lax.rem(row + 2, ROWS)

    def at_y(d):
        return lax.rem(y + d + NY, NY)

    def at_z(d):
        return lax.rem(z + d + NZ, NZ)

    def col_of(yy, zz):
        return {"col": yy * NZ + zz}

    def remote(ref, ssem, rsem, target):
        return pltpu.make_async_remote_copy(
            src_ref=ref, dst_ref=ref, send_sem=ssem, recv_sem=rsem,
            device_id=target, device_id_type=MESH,
        )

    def halved(d, first, count):
        cut = count // 2
        return (first, cut) if d == 1 else (first + cut, count - cut)

    def part(yy, zz, c, first, count):
        return gathered.at[yy, zz, pl.ds((c * tiles + first) * 8, count * 8), :]

    def a1(c, d, h, arriving):
        zz = at_z(-d * (h if arriving else h - 1))
        span = halved(d, 0, tiles_a) if h == 4 else (0, tiles_a)
        k = (0 if d == 1 else 4) + h - 1
        return remote(part(y, zz, c, *span), s_a1.at[c, k], r_a1.at[c, k], col_of(y, at_z(d)))

    def line(c, d, far_z, arriving):
        yy = at_y(-d if arriving else 0)
        zz = at_z(far_z)
        k = (0 if d == 1 else NZ + 1) + far_z % NZ
        return remote(
            part(yy, zz, c, 0, tiles_a), s_a2.at[c, k], r_a2.at[c, k], col_of(at_y(d), z)
        )

    def onward(c, d, arriving):
        yy = at_y(-d * (2 if arriving else 1))
        zz = pl.ds(*halved(d, 0, NZ))
        k = (0 if d == 1 else NZ + 1) + NZ
        return remote(
            part(yy, zz, c, 0, tiles_a), s_a2.at[c, k], r_a2.at[c, k], col_of(at_y(d), z)
        )

    def spread(*far_z):
        def act(c):
            for k in far_z:
                for d in (1, -1):
                    line(c, d, k, False).start()

        return act

    def a2_on(c):
        for d in (1, -1):
            for k in range(NZ):
                line(c, d, k, True).wait_recv()
            onward(c, d, False).start()

    def a2_end(c):
        for d in (1, -1):
            onward(c, d, True).wait_recv()

    def a2_sent(c):
        for d in (1, -1):
            for k in range(NZ):
                line(c, d, k, False).wait_send()
            onward(c, d, False).wait_send()

    def b1(c, d, h, arriving):
        yy = at_y(-d * (h if arriving else h - 1))
        span = halved(d, tiles_a, tiles_b) if h == 2 else (tiles_a, tiles_b)
        k = (0 if d == 1 else 2) + h - 1
        return remote(part(yy, z, c, *span), s_b1.at[c, k], r_b1.at[c, k], col_of(at_y(d), z))

    def b2(c, d, h, arriving):
        zz = at_z(-d * (h if arriving else h - 1))
        yy = pl.ds(*(halved(d, 0, NY) if h == 4 else (0, NY)))
        k = (0 if d == 1 else 4) + h - 1
        return remote(
            part(yy, zz, c, tiles_a, tiles_b), s_b2.at[c, k], r_b2.at[c, k], col_of(y, at_z(d))
        )

    def begin(what, c):
        for d in (1, -1):
            what(c, d, 1, False).start()

    def forward(what, c, h):
        for d in (1, -1):
            what(c, d, h, True).wait_recv()
            what(c, d, h + 1, False).start()

    def arrive(what, c, h):
        for d in (1, -1):
            what(c, d, h, True).wait_recv()

    def sent(what, c, hops):
        for d in (1, -1):
            for h in range(1, hops + 1):
                what(c, d, h, False).wait_send()

    u_own_sib = remote(ug.at[row], s_u.at[0], r_u.at[0], {"row": sib})
    u_own_far = remote(ug.at[row], s_u.at[1], r_u.at[1], {"row": far})
    u_fwd = remote(ug.at[far], s_u.at[2], r_u.at[2], {"row": sib})
    far_sib = lax.rem(sib + 2, ROWS)

    def u_arrive(k, which):
        remote(ug.at[which], s_u.at[k], r_u.at[k], {"row": sib}).wait_recv()

    def exchange(c):
        return pltpu.make_async_remote_copy(
            src_ref=mine.at[c], dst_ref=rx_ref.at[c], send_sem=s_x.at[c], recv_sem=r_x.at[c],
            device_id={"layer": 1 - layer}, device_id_type=MESH,
        )

    def store_out(c):
        return pltpu.make_async_copy(mine.at[c], mine_ref.at[c], l_out.at[c])

    load_anc = pltpu.make_async_copy(anc_ref, anc, l_anc)
    load_anc.start()

    barrier = pltpu.get_barrier_semaphore()
    greeted = [
        {"row": sib}, {"row": far}, {"layer": 1 - layer},
        col_of(at_y(1), z), col_of(at_y(-1), z), col_of(y, at_z(1)), col_of(y, at_z(-1)),
    ]
    for other in greeted:
        pl.semaphore_signal(barrier, inc=1, device_id=other, device_id_type=MESH)

    for panel in range(PANELS):
        ug[row, panel * 128 : panel * 128 + 128, :] = up_ref[0, panel]
    ug[row, PANELS * 128 :, :] = fu_ref[...]

    for r in range(BLOCKS):
        lanes = slice(r * BLK, r * BLK + BLK)
        for q in range(TILES - 1):
            own[r * TILES + q] = low_ref[q, :, lanes]
        own[r * TILES + TILES - 1] = fl_ref[:, lanes]
    high[0] = jnp.zeros(high.shape[1:], BF16)
    low[0] = jnp.zeros(low.shape[1:], BF16)

    def place(c):
        for n in range(tiles):
            t = c * tiles + n
            gathered[y, z, pl.ds(t * 8, 8), :] = own[tab_ref[SOURCE + t // BLK, lax.rem(t, BLK)]]

    def unpack(c):
        for n in range(tiles):
            t = c * tiles + n
            piece = gathered[:, :, pl.ds(t * 8, 8), :].reshape(256, BLK)
            high[t + 1], low[t + 1] = split(piece)

    pl.semaphore_wait(barrier, len(greeted))

    u_own_far.start()
    u_own_sib.start()

    def scale(mask_ref, *index):
        return mask_ref[index].astype(F32)

    def convert_upper(r):
        for half in range(2):
            cols = slice(half * BLK, half * BLK + BLK)
            beside = slice((2 + half) * BLK, (3 + half) * BLK)
            for panel in range(PANELS):
                keep = scale(ub_ref, 0, panel, col * 2 + half)
                for odd in range(2):
                    for pair in range(4):
                        at = panel * 128 + pair * 32 + odd * 8
                        both = jnp.concatenate(
                            [ug[r, at : at + 8, cols], ug[r, at + 16 : at + 24, cols]], axis=0
                        )
                        above, below = split(both * keep)
                        to = pl.ds(pl.multiple_of(r * 64 + pair * 16, 16), 16)
                        upper[panel * 2 + odd, to, cols] = above
                        upper[panel * 2 + odd, to, beside] = below
            keep = scale(fub_ref, col * 2 + half)
            above, below = split(ug[r, PANELS * 128 :, cols] * keep)
            to = pl.ds(pl.multiple_of(r * 64, 64), 64)
            upper[TILES - 1, to, cols] = above
            upper[TILES - 1, to, beside] = below

    def compute(c, r):
        at = row * BLOCKS + c * R + r
        total = anc[tab_ref[ORDER, at]]
        for q in range(TILES):
            t = tab_ref[T_OF + q, at]
            total = total - contract(high[t], low[t], upper, q)
        mine[c * R + r] = total

    def upper_near(c):
        @pl.when(c == 0)
        def _():
            load_anc.wait()
            convert_upper(row)
            u_arrive(0, sib)
            convert_upper(sib)

    def upper_far(c):
        @pl.when(c == 0)
        def _():
            u_arrive(1, far)
            u_fwd.start()
            convert_upper(far)

    def upper_last(c):
        @pl.when(c == 0)
        def _():
            u_arrive(2, far_sib)
            convert_upper(far_sib)

    def work(c):
        unpack(c)
        for r in range(R):
            compute(c, r)
            exchange(c * R + r).start()
            store_out(c * R + r).start()

    def clear(c):
        sent(a1, c, 4)
        sent(b1, c, 2)
        a2_sent(c)
        sent(b2, c, 4)

    def starts(what):
        return lambda c: begin(what, c)

    def moves(what, hop):
        return lambda c: forward(what, c, hop)

    def ends(what, hop):
        return lambda c: arrive(what, c, hop)

    def step(i, _):
        def run(offset, *actions):
            @pl.when((i >= offset) & (i < chunks + offset))
            def _():
                for action in actions:
                    action(i - offset)

        run(0, place, starts(a1), starts(b1), spread(0))
        run(1, moves(a1, 1), moves(b1, 1), spread(1, -1))
        run(2, moves(a1, 2), ends(b1, 2), starts(b2), spread(2, -2))
        run(2, upper_near)
        run(3, moves(a1, 3), moves(b2, 1), spread(3, -3))
        run(4, ends(a1, 4), spread(4), moves(b2, 2))
        run(4, upper_far)
        run(5, a2_on, moves(b2, 3))
        run(6, upper_last, a2_end, ends(b2, 4), work)
        run(7, clear)
        return 0

    lax.fori_loop(0, chunks + 8, step, 0)
    u_own_sib.wait_send()
    u_own_far.wait_send()
    u_fwd.wait_send()

    def drain(c, _):
        exchange(c).wait()
        store_out(c).wait()
        return 0

    lax.fori_loop(0, BLOCKS, drain, 0)


def tables(lb_ref, flb_ref, tab_ref, size_ref, mask, other, sent, came):
    layer = lax.axis_index("layer")
    row = lax.axis_index("row")
    barrier = pltpu.get_barrier_semaphore()
    target = {"layer": 1 - layer}
    pl.semaphore_signal(barrier, inc=1, device_id=target, device_id_type=MESH)
    mask[...] = jnp.zeros_like(mask)
    mask[0:PANELS, 0:64] = lb_ref[0].astype(F32)
    mask[PANELS : PANELS + 1, 0:64] = flb_ref[...].astype(F32)
    pl.semaphore_wait(barrier, 1)
    copy = pltpu.make_async_remote_copy(
        src_ref=mask, dst_ref=other, send_sem=sent, recv_sem=came,
        device_id=target, device_id_type=MESH,
    )
    copy.start()
    square = (BLK, BLK)
    sub = lax.broadcasted_iota(jnp.int32, square, 0)
    lane = lax.broadcasted_iota(jnp.int32, square, 1)
    same = ((sub >> 4) == (lane >> 4)).astype(F32)
    earlier = (sub < lane).astype(F32)

    def ranked(held):
        weight = 2.0 * jnp.sum(held[0:PANELS], axis=0, keepdims=True) + held[PANELS : PANELS + 1]
        here = jnp.broadcast_to(weight, square)
        there = here.T
        before = jnp.where(there < here, 1.0, jnp.where(there == here, earlier, 0.0)) * same
        place = jnp.sum(before, axis=0, keepdims=True)
        start = jnp.sum(before * there, axis=0, keepdims=True)
        most = jnp.max(jnp.sum(same * there, axis=0, keepdims=True), axis=1, keepdims=True)
        return place, start, most

    held = mask[...]
    place, start, most = ranked(held)
    has = [held[min(q // 2, PANELS) : min(q // 2, PANELS) + 1] for q in range(TILES)]
    spots = []
    for q in range(TILES):
        spots.append(start)
        start = start + has[q]
    ours = ((lax.broadcasted_iota(jnp.int32, (1, BLK), 1) >> 4) == row).astype(F32)
    rows = [h * ours * (spot + 1.0) - 1.0 for h, spot in zip(has, spots)] + [place]
    turned = jnp.concatenate(rows + [jnp.zeros((BLK - TILES - 1, BLK), F32)], axis=0).T
    lane_f = lane.astype(F32)
    within = (sub & 15).astype(F32)
    hit = jnp.where(turned[:, TILES : TILES + 1] == (lane & 15).astype(F32), same, 0.0)
    source = [jnp.zeros(square, F32) for _ in range(2)]
    for q in range(TILES):
        spot = turned[:, q : q + 1]
        code = within * float(TILES) + float(q)
        for part in range(2):
            source[part] = source[part] + jnp.where(spot == lane_f + float(part * BLK), code, 0.0)
    moved = [h * (spot + 1.0) for h, spot in zip(has, spots)]
    moved.append((lax.broadcasted_iota(jnp.int32, (1, BLK), 1) & 15).astype(F32))
    moved = jnp.concatenate(moved + [jnp.zeros((16 - len(moved), BLK), F32)], axis=0)
    moved = jnp.dot(moved, hit, precision=lax.Precision.HIGHEST, preferred_element_type=F32)
    out = [jnp.sum(value, axis=0, keepdims=True) for value in source]
    out.append(place)
    copy.wait()
    place_other, _, most_other = ranked(other[...])
    out.append(place_other)
    most = jnp.max(jnp.maximum(most, most_other)).astype(jnp.int32)
    size = jnp.int32(0)
    for tiles, _ in SIZES[:-1]:
        size = size + (most > tiles * CHUNKS).astype(jnp.int32)
    size_ref[0] = size
    tab_ref[0:TILES + 1, :] = (moved[0:TILES + 1] + 0.5).astype(jnp.int32)
    for n, value in enumerate(out):
        tab_ref[SOURCE + n : SOURCE + n + 1, :] = value.astype(jnp.int32)
    tab_ref[POS_OTHER + 1 :, :] = jnp.zeros((15 - POS_OTHER, BLK), jnp.int32)


def combine(tab_ref, mine_ref, rx_ref, out_ref, total, sem_o):
    row = lax.axis_index("row")

    def store(n):
        return pltpu.make_async_copy(total.at[n], out_ref.at[n], sem_o.at[n])

    for n in range(BLOCKS):
        at = row * BLOCKS + n
        total[n] = mine_ref[tab_ref[POS, at]] + rx_ref[tab_ref[POS_OTHER, at]]
        store(n).start()
    for n in range(BLOCKS):
        store(n).wait()


VMEM = pl.BlockSpec(memory_space=pltpu.VMEM)
SMEM = pl.BlockSpec(memory_space=pltpu.SMEM)
HBM = pl.BlockSpec(memory_space=pl.ANY)


def gather_update(n, cols, rows):
    tiles, tiles_a = SIZES[n]
    dma = pltpu.SemaphoreType.DMA
    result = jax.ShapeDtypeStruct((BLOCKS, BLK, cols), F32)
    return pl.pallas_call(
        functools.partial(kernel, tiles, tiles_a),
        out_shape=(result, result),
        in_specs=[SMEM, HBM, VMEM, VMEM, SMEM, VMEM, VMEM, SMEM],
        out_specs=(HBM, HBM),
        scratch_shapes=[
            pltpu.VMEM((NY, NZ, CHUNKS * tiles * 8, BLK), F32),
            pltpu.VMEM((BLOCKS * TILES, 8, BLK), F32),
            pltpu.VMEM((CHUNKS * tiles + 1, 256, BLK), BF16),
            pltpu.VMEM((CHUNKS * tiles + 1, 256, BLK), BF16),
            pltpu.VMEM((ROWS, PANELS * 128 + 64, cols), F32),
            pltpu.VMEM((TILES, 256, 2 * cols), BF16),
            pltpu.VMEM((BLOCKS, BLK, cols), F32),
            pltpu.VMEM((BLOCKS, BLK, cols), F32),
            dma((CHUNKS, 8)), dma((CHUNKS, 8)),
            dma((CHUNKS, 18)), dma((CHUNKS, 18)),
            dma((CHUNKS, 4)), dma((CHUNKS, 4)),
            dma((CHUNKS, 8)), dma((CHUNKS, 8)),
            dma((3,)), dma((3,)),
            dma((BLOCKS,)), dma((BLOCKS,)),
            dma, dma((BLOCKS,)),
        ],
        compiler_params=pltpu.CompilerParams(
            collective_id=n + 1, has_side_effects=True, vmem_limit_bytes=56 << 20
        ),
        name="gather_update_exchange",
    )


def body(anc, low, up, lb, ub, fl, fu, flb, fub):
    rows, cols = anc.shape[1:]
    dma = pltpu.SemaphoreType.DMA
    tab, size = pl.pallas_call(
        tables,
        out_shape=(
            jax.ShapeDtypeStruct((16, BLK), jnp.int32), jax.ShapeDtypeStruct((1,), jnp.int32)
        ),
        in_specs=[VMEM, VMEM],
        out_specs=(VMEM, SMEM),
        scratch_shapes=[pltpu.VMEM((8, BLK), F32), pltpu.VMEM((8, BLK), F32), dma, dma],
        compiler_params=pltpu.CompilerParams(collective_id=0, has_side_effects=True),
        name="block_tables",
    )(lb, flb.reshape(1, -1))
    mine, rx = lax.switch(
        size[0],
        [gather_update(n, cols, rows) for n in range(len(SIZES))],
        tab, anc.reshape(BLOCKS, BLK, cols), low.reshape(2 * PANELS, 8, rows), up, ub, fl, fu, fub,
    )
    blocks = (BLOCKS, BLK, cols)
    out = pl.pallas_call(
        combine,
        out_shape=jax.ShapeDtypeStruct(blocks, F32),
        in_specs=[SMEM, VMEM, VMEM],
        out_specs=HBM,
        scratch_shapes=[pltpu.VMEM(blocks, F32), dma((BLOCKS,))],
        compiler_params=pltpu.CompilerParams(vmem_limit_bytes=16 << 20),
        name="layer_sum",
    )(tab, mine, rx)
    return out.reshape(rows, cols)


def solution(mesh):
    return jax.shard_map(
        body,
        mesh=mesh,
        in_specs=(
            P("layer", "row", "col"),
            P("layer", None, "col", "row"),
            P("layer", None, "row", "col"),
            P("layer", None, None),
            P("layer", None, None),
            P(("layer", "col"), "row"),
            P(("layer", "row"), "col"),
            P(),
            P(),
        ),
        out_specs=P("row", "col"),
        check_vma=False,
    )
```
